128 devices in a mesh: cell: 64 (over x, y, z_lo, core), rank: 2 (over z_hi).
Axes of the slice: x: 4, y: 4, z: 4 (z_hi: 2, z_lo: 2; z = z_hi * 2 + z_lo), core: 2. Of those that a mesh axis runs over, the one named last changes fastest.
Arguments:
- factors: float32 [48, 256, 2048], P(None, 'cell', 'rank'), may hold values from -1.7 to 1.7
- rank_weights: float32 [2048], P('rank'), may hold values from 0.5 to 2
- triples: int32 [2, 3], replicated, may hold values from 0 to 47, as said below
- targets: bfloat16 [2, 256, 256, 256], P(None, 'cell'), may hold values from -6 to 6
Outputs:
- new_factors: float32 [48, 256, 2048], P(None, 'cell', 'rank')
The draws below stay inside these ranges and needn't reach their ends.
Inputs may be any that keep to these rules, and one draw needn't show every extreme that they name: `triples`: the three attributes of a table are different.
All inputs are finite; a program needn't handle non-finite values.
Results may differ from the reference program's by a relative error of at most 0.0022.
Values may be sent and summed in bfloat16 or wider, within the bound.
A program may use at most 64 MiB of HBM per device.

```python
import math
import jax
import jax.numpy as jnp
from jax import lax

ATTRS = 48
LEVELS = 256
RANK = 2048
TABLES = 2


def pick_three(subkey):
    return jax.random.permutation(subkey, ATTRS)[:3]


def draw_triples(key, part):
    key = jax.random.fold_in(key, 7)
    table_key, middle_key, order_key, which_key = jax.random.split(key, 4)
    table_keys = jax.random.split(table_key, TABLES)
    chosen = jax.vmap(pick_three)(table_keys).astype(jnp.int32)
    middle = jax.random.randint(middle_key, (1,), 1, ATTRS - 1).astype(jnp.int32)
    special = jnp.concatenate([jnp.zeros((1,), jnp.int32), jnp.full((1,), ATTRS - 1, jnp.int32), middle])
    special = jax.random.permutation(order_key, special)
    which = jax.random.randint(which_key, (), 0, TABLES).astype(jnp.int32)
    rows = jnp.arange(TABLES, dtype=jnp.int32)
    chosen = jnp.where((rows == which)[:, None], special[None, :], chosen)
    return chosen.astype(jnp.int32)


def level_of(stream_key, dims, pieces, least, largest):
    factor_of = 1.0
    for dim, shards_of in pieces:
        heights = jax.random.uniform(jax.random.fold_in(jax.random.fold_in(stream_key, 6), dim), (shards_of,), jnp.float32, least / len(pieces), largest / len(pieces))
        factor_of = factor_of * jnp.repeat(jnp.exp(heights), dims[dim] // shards_of).reshape((-1,) + (1,) * (len(dims) - 1 - dim))
    return factor_of


def bell_draw(key, extent, scale, limit, pieces=(), kind=jnp.bfloat16):
    loudness = level_of(key, extent, pieces, -0.22, 0.18) if pieces else 1.0
    array = jax.random.normal(key, extent, jnp.float32) * scale * loudness
    return jnp.minimum(jnp.maximum(array, -limit), limit).astype(kind)


def setup_inputs(seed: int = 0) -> dict:
    key_of = jax.random.split(jax.random.key(seed), 5)
    factors = bell_draw(key_of[0], (ATTRS, LEVELS, RANK), 0.28, 1.7, ((1, 64), (2, 2)), jnp.float32)
    rank_weights = jnp.clip(jnp.exp(math.log(2.0) - 1.3862944 * jax.random.uniform(key_of[1], (RANK,), jnp.float32) ** level_of(key_of[1], (RANK,), ((0, 2),), -0.2, 0.2)), 0.5, 2.0)
    triples = draw_triples(jax.random.fold_in(key_of[4], 71), 0)
    targets = bell_draw(key_of[3], (TABLES, LEVELS, LEVELS, LEVELS), 1.0, 6.0, ((1, 64),))
    return {"factors": factors, "rank_weights": rank_weights, "triples": triples, "targets": targets}


learn_rate = 0.02


def table_terms(factors, rank_weights, first_attr, second_attr, third_attr, table_target):
    full_first = factors[first_attr]
    full_second = factors[second_attr]
    full_third = factors[third_attr]
    second_bf = full_second.astype(jnp.bfloat16)
    third_bf = full_third.astype(jnp.bfloat16)

    def per_level(carry, inputs):
        grad_second, grad_third = carry
        first_row, target_slab = inputs
        scaled = (rank_weights * first_row * full_second).astype(jnp.bfloat16)
        model = jnp.dot(scaled, third_bf.T, preferred_element_type=jnp.float32)
        resid = (model - target_slab.astype(jnp.float32)).astype(jnp.bfloat16)
        xprod = jnp.dot(resid, third_bf, preferred_element_type=jnp.float32)
        vprod = jnp.dot(resid.T, second_bf, preferred_element_type=jnp.float32)
        grad_row = rank_weights * jnp.sum(xprod * full_second, axis=0)
        grad_second = grad_second + rank_weights * first_row * xprod
        grad_third = grad_third + rank_weights * first_row * vprod
        return (grad_second, grad_third), grad_row

    zeros_init = jnp.zeros(full_second.shape, jnp.float32)
    (grad_second, grad_third), grad_first = lax.scan(per_level, (zeros_init, zeros_init), (full_first, table_target))
    return grad_first, grad_second, grad_third


def reference(factors, rank_weights, triples, targets):
    gradient = jnp.zeros(factors.shape, jnp.float32)
    for table in range(TABLES):
        first_attr = triples[table, 0]
        second_attr = triples[table, 1]
        third_attr = triples[table, 2]
        grad_first, grad_second, grad_third = table_terms(factors, rank_weights, first_attr, second_attr, third_attr, targets[table])
        gradient = gradient.at[first_attr].add(grad_first)
        gradient = gradient.at[second_attr].add(grad_second)
        gradient = gradient.at[third_attr].add(grad_third)
    return factors - learn_rate * gradient
```

```python
import functools

import jax
import jax.numpy as jnp
from jax import lax
from jax.experimental import pallas as pl
from jax.experimental.pallas import tpu as pltpu
from jax.sharding import PartitionSpec as P

learn_rate = 0.02
MESH = pl.DeviceIdType.MESH
f32, bf16 = jnp.float32, jnp.bfloat16


def cell_of(x, y, zl, core):
    return ((x * 4 + y) * 2 + zl) * 2 + core


def rcopy(src, dst, send_sem, recv_sem, cell, rank):
    return pltpu.make_async_remote_copy(
        src_ref=src, dst_ref=dst, send_sem=send_sem, recv_sem=recv_sem,
        device_id={"cell": cell, "rank": rank}, device_id_type=MESH)


def kernel(tri, w, fac, tgt, out, msg, col, bfull, cfull, wa, tg, scaled, pm_own, pm_send, pm_recv, ga, gb, gc,
           gb_send, gc_send, b1, c1, b1_send, c1_send, b2, c2, fsend, frecv, full,
           t_local, t_sem, col_s, col_r, g1_s, g1_r, g2_s, g2_r, pm_s, pm_r, r1_s, r1_r, r2_s, r2_r, f_s, f_r):
    cell = lax.axis_index("cell")
    zh = lax.axis_index("rank")
    core = cell % 2
    zl = (cell // 2) % 2
    y = (cell // 4) % 4
    x = cell // 16
    rows = w.shape[1]

    barrier = pltpu.get_barrier_semaphore()
    for dz in range(2):
        for dl in range(2):
            for dc in range(2):
                if dz or dl or dc:
                    pl.semaphore_signal(
                        barrier, inc=1, device_id_type=MESH,
                        device_id={"cell": cell_of(x, y, (zl + dl) % 2, (core + dc) % 2), "rank": (zh + dz) % 2})
    for d in range(1, 4):
        pl.semaphore_signal(barrier, inc=1, device_id_type=MESH,
                            device_id={"cell": cell_of((x + d) % 4, y, zl, core), "rank": zh})
        pl.semaphore_signal(barrier, inc=1, device_id_type=MESH,
                            device_id={"cell": cell_of(x, (y + d) % 4, zl, core), "rank": zh})

    own_tgt = pltpu.make_async_copy(tgt.at[zh], tg.at[pl.ds(core * 4, 4)], t_local)
    own_tgt.start()
    for t in range(2):
        a = w[...] * fac[tri[t, 0]]
        b = fac[tri[t, 1]]
        c = fac[tri[t, 2]]
        hi = a.astype(bf16).astype(f32)
        msg[t] = jnp.concatenate([hi, b, c, a - hi], axis=0).astype(bf16)
    pl.semaphore_wait(barrier, 13)

    slot = zl * 2 + core
    for t in range(2):
        for dl in range(2):
            to_l = (zl + dl) % 2
            is_self = (dl == 0) & (core == zh) & (zh == t)

            @pl.when(jnp.logical_not(is_self))
            def _():
                rcopy(msg.at[t], col.at[slot], col_s.at[t * 2 + dl], col_r.at[slot], cell_of(x, y, to_l, zh), t).start()

            if dl == 0:
                @pl.when(is_self)
                def _():
                    col[slot] = msg[t]
    tg_copy = rcopy(tgt.at[zh], tg.at[pl.ds(core * 4, 4)], t_sem.at[0], t_sem.at[1], cell_of(x, y, zl, 1 - core), zh)
    tg_copy.start()
    for s in range(4):
        from_self = (core == zh) & (slot == s)

        @pl.when(jnp.logical_not(from_self))
        def _():
            rcopy(msg.at[0], col.at[s], col_s.at[0], col_r.at[s], cell_of(x, y, zl, 1 - core), zh).wait_recv()
    got = [col[s].astype(f32) for s in range(4)]
    bfull[x, y] = jnp.concatenate([m[4:8] for m in got], axis=0).astype(bf16)
    cfull[x, y] = jnp.concatenate([m[8:12] for m in got], axis=0).astype(bf16)
    own = [col[zl * 2 + c].astype(f32) for c in range(2)]
    wa[...] = jnp.concatenate([m[0:4] + m[12:16] for m in own], axis=0)

    first = []
    for d in range(1, 4):
        first.append(rcopy(bfull.at[x, y], bfull.at[x, y], g1_s.at[d], g1_r.at[d], cell_of((x + d) % 4, y, zl, core), zh))
        first.append(rcopy(cfull.at[x, y], cfull.at[x, y], g1_s.at[4 + d], g1_r.at[4 + d], cell_of(x, (y + d) % 4, zl, core), zh))
    for copy in first:
        copy.start()
    for d in range(1, 4):
        bx, cy = (x + 4 - d) % 4, (y + 4 - d) % 4
        rcopy(bfull.at[bx, y], bfull.at[bx, y], g1_s.at[d], g1_r.at[d], cell_of(bx, y, zl, core), zh).wait_recv()
        rcopy(cfull.at[x, cy], cfull.at[x, cy], g1_s.at[4 + d], g1_r.at[4 + d], cell_of(x, cy, zl, core), zh).wait_recv()
    for copy in first:
        copy.wait_send()

    up_y, dn_y = cell_of(x, (y + 1) % 4, zl, core), cell_of(x, (y + 3) % 4, zl, core)
    up_x, dn_x = cell_of((x + 1) % 4, y, zl, core), cell_of((x + 3) % 4, y, zl, core)

    def half(ref, which, part, h):
        return ref.at[pl.ds(2 * h, 2), part] if which == 0 else ref.at[part, pl.ds(2 * h, 2)]

    def second(which, k, part, h, to):
        ref = (bfull, cfull)[which]
        view = half(ref, which, part, h)
        return rcopy(view, view, g2_s.at[which * 6 + k], g2_r.at[which * 6 + k], to, zh)

    pos = (y, x)
    ups, dns = (up_y, up_x), (dn_y, dn_x)
    sent = []
    for k in range(2):
        for which in range(2):
            sent.append(second(which, k, pos[which], k, ups[which]))
            sent.append(second(which, 2 + k, pos[which], 1 - k, dns[which]))
    for copy in sent:
        copy.start()
    forwards = []
    for which in range(2):
        below, above = (pos[which] + 3) % 4, (pos[which] + 1) % 4
        second(which, 0, below, 0, dns[which]).wait_recv()
        forwards.append(second(which, 4, below, 0, ups[which]))
        forwards[-1].start()
        second(which, 2, above, 1, ups[which]).wait_recv()
        forwards.append(second(which, 5, above, 1, dns[which]))
        forwards[-1].start()
    for which in range(2):
        below, above, far = (pos[which] + 3) % 4, (pos[which] + 1) % 4, (pos[which] + 2) % 4
        second(which, 1, below, 1, dns[which]).wait_recv()
        second(which, 3, above, 0, ups[which]).wait_recv()
        second(which, 4, far, 0, dns[which]).wait_recv()
        second(which, 5, far, 1, ups[which]).wait_recv()
    for copy in sent + forwards:
        copy.wait_send()

    other = cell_of(x, y, zl, 1 - core)

    def pm_copy(i):
        return rcopy(pm_send.at[i], pm_recv.at[i], pm_s.at[i], pm_r.at[i], other, zh)

    @pl.loop(0, 8)
    def _(i):
        s = (wa[pl.ds(i, 1), :] * bfull[...].reshape(256, rows).astype(f32)).astype(bf16)
        scaled[i] = s
        pm = lax.dot_general(s, cfull[...].reshape(256, rows), (((1,), (1,)), ((), ())), preferred_element_type=f32)
        pm_own[i] = pm
        pm_send[i] = pm.astype(bf16)
        pm_copy(i).start()

    own_tgt.wait()
    tg_copy.wait_send()
    rcopy(tgt.at[zh], tg.at[pl.ds((1 - core) * 4, 4)], t_sem.at[0], t_sem.at[1], other, zh).wait_recv()

    gb[...] = jnp.zeros_like(gb)
    gc[...] = jnp.zeros_like(gc)

    @pl.loop(0, 8)
    def _(i):
        pm_copy(i).wait_recv()
        r = (pm_own[i] + pm_recv[i].astype(f32) - tg[i].astype(f32)).astype(bf16)
        xprod = jnp.dot(r, cfull[...].reshape(256, rows), preferred_element_type=f32)
        ga[pl.ds(i, 1), :] = jnp.sum(xprod * bfull[...].reshape(256, rows).astype(f32), axis=0, keepdims=True)
        gb[...] += wa[pl.ds(i, 1), :] * xprod
        gc[...] += lax.dot_general(r, scaled[i], (((0,), (0,)), ((), ())), preferred_element_type=f32)

    @pl.loop(0, 8)
    def _(i):
        pm_copy(i).wait_send()

    gb_send[...] = gb[...].reshape(4, 4, 16, rows).astype(bf16)
    gc_send[...] = gc[...].reshape(4, 4, 16, rows).astype(bf16)
    first = []
    for d in range(1, 4):
        ty, tx = (y + d) % 4, (x + d) % 4
        first.append(rcopy(gb_send.at[:, ty], b1.at[d - 1], r1_s.at[d], r1_r.at[d], cell_of(x, ty, zl, core), zh))
        first.append(rcopy(gc_send.at[tx], c1.at[d - 1], r1_s.at[4 + d], r1_r.at[4 + d], cell_of(tx, y, zl, core), zh))
    for copy in first:
        copy.start()
    for copy in first:
        copy.wait_recv()
    for q in range(4):
        @pl.when(y == q)
        def _():
            full[0] = gb[...].reshape(4, 4, 16, rows)[:, q]

        @pl.when(x == q)
        def _():
            full[1] = gc[...].reshape(4, 4, 16, rows)[q]
    full[0] += b1[0].astype(f32) + b1[1].astype(f32) + b1[2].astype(f32)
    full[1] += c1[0].astype(f32) + c1[1].astype(f32) + c1[2].astype(f32)
    b1_send[...] = full[0].astype(bf16)
    c1_send[...] = full[1].astype(bf16)
    for copy in first:
        copy.wait_send()
    last = []
    for d in range(1, 4):
        ty, tx = (y + d) % 4, (x + d) % 4
        last.append(rcopy(b1_send.at[tx], b2.at[d - 1], r2_s.at[d], r2_r.at[d], cell_of(tx, y, zl, core), zh))
        last.append(rcopy(c1_send.at[ty], c2.at[d - 1], r2_s.at[4 + d], r2_r.at[4 + d], cell_of(x, ty, zl, core), zh))
    for copy in last:
        copy.start()
    for copy in last:
        copy.wait_recv()
    sum_b = full[0, x] + b2[0].astype(f32) + b2[1].astype(f32) + b2[2].astype(f32)
    sum_c = full[1, y] + c2[0].astype(f32) + c2[1].astype(f32) + c2[2].astype(f32)
    for copy in last:
        copy.wait_send()

    grad_a = ga[...]
    for s in range(4):
        c = s % 2
        ga4 = grad_a[4 * c:4 * c + 4]
        ga4 = jnp.where(zl == s // 2, ga4, 0.0)
        fsend[s] = jnp.concatenate([sum_b[4 * s:4 * s + 4], sum_c[4 * s:4 * s + 4], ga4, jnp.zeros_like(ga4)], axis=0)
    fslot = zl * 2 + zh
    for s in range(4):
        is_self = (slot == s) & (zh == core)

        @pl.when(jnp.logical_not(is_self))
        def _():
            rcopy(fsend.at[s], frecv.at[fslot], f_s.at[s], f_r.at[fslot], cell_of(x, y, s // 2, s % 2), core).start()

        @pl.when(is_self)
        def _():
            frecv[fslot] = fsend[s]
    for s in range(4):
        from_self = (fslot == s) & (zh == core)

        @pl.when(jnp.logical_not(from_self))
        def _():
            rcopy(fsend.at[0], frecv.at[s], f_s.at[0], f_r.at[s], other, zh).wait_recv()
    grads = []
    for t in range(2):
        g = learn_rate * (frecv[t] + frecv[2 + t])
        grads.append((tri[t, 0], w[...] * g[8:12]))
        grads.append((tri[t, 1], g[0:4]))
        grads.append((tri[t, 2], g[4:8]))

    @pl.loop(0, 48)
    def _(attr):
        step = jnp.zeros((4, rows), f32)
        for which, g in grads:
            step = step + jnp.where(which == attr, g, 0.0)
        out[attr] = fac[attr] - step

    for t in range(2):
        for dl in range(2):
            is_self = (dl == 0) & (core == zh) & (zh == t)

            @pl.when(jnp.logical_not(is_self))
            def _():
                rcopy(msg.at[t], col.at[slot], col_s.at[t * 2 + dl], col_r.at[slot], other, t).wait_send()
    for s in range(4):
        is_self = (slot == s) & (zh == core)

        @pl.when(jnp.logical_not(is_self))
        def _():
            rcopy(fsend.at[s], frecv.at[fslot], f_s.at[s], f_r.at[fslot], other, core).wait_send()


def on_device(factors, rank_weights, triples, targets):
    rows = rank_weights.shape[0]
    vmem = pl.BlockSpec(memory_space=pltpu.VMEM)
    dma = pltpu.SemaphoreType.DMA
    V = pltpu.VMEM
    return pl.pallas_call(
        kernel,
        out_shape=jax.ShapeDtypeStruct(factors.shape, f32),
        in_specs=[pl.BlockSpec(memory_space=pltpu.SMEM), vmem, vmem, pl.BlockSpec(memory_space=pl.ANY)],
        out_specs=vmem,
        scratch_shapes=[
            V((2, 16, rows), bf16),
            V((4, 16, rows), bf16),
            V((4, 4, 16, rows), bf16),
            V((4, 4, 16, rows), bf16),
            V((8, rows), f32),
            V((8, 256, 256), bf16),
            V((8, 256, rows), bf16),
            V((8, 256, 256), f32),
            V((8, 256, 256), bf16),
            V((8, 256, 256), bf16),
            V((8, rows), f32),
            V((256, rows), f32),
            V((256, rows), f32),
            V((4, 4, 16, rows), bf16),
            V((4, 4, 16, rows), bf16),
            V((3, 4, 16, rows), bf16),
            V((3, 4, 16, rows), bf16),
            V((4, 16, rows), bf16),
            V((4, 16, rows), bf16),
            V((3, 16, rows), bf16),
            V((3, 16, rows), bf16),
            V((4, 16, rows), f32),
            V((4, 16, rows), f32),
            V((2, 4, 16, rows), f32),
            dma, dma((2,)), dma((4,)), dma((4,)), dma((8,)), dma((8,)), dma((12,)), dma((12,)),
            dma((8,)), dma((8,)), dma((8,)), dma((8,)), dma((8,)), dma((8,)), dma((4,)), dma((4,)),
        ],
        compiler_params=pltpu.CompilerParams(collective_id=0, has_side_effects=True, vmem_limit_bytes=56 * 1024 * 1024),
    )(triples, rank_weights.reshape(1, rows), factors, targets)


def solution(mesh):
    in_specs = (P(None, "cell", "rank"), P("rank"), P(), P(None, "cell", None, None))
    return jax.shard_map(on_device, mesh=mesh, in_specs=in_specs, out_specs=P(None, "cell", "rank"), check_vma=False)
```

```python
import jax
import jax.numpy as jnp
from jax import lax
from jax.experimental import pallas as pl
from jax.experimental.pallas import tpu as pltpu
from jax.sharding import PartitionSpec as P

learn_rate = 0.02
MESH = pl.DeviceIdType.MESH
f32, bf16 = jnp.float32, jnp.bfloat16
NT = (((1,), (1,)), ((), ()))


def cell_of(x, y, zl, core):
    return ((x * 4 + y) * 2 + zl) * 2 + core


def rcopy(src, dst, send_sem, recv_sem, cell, rank):
    return pltpu.make_async_remote_copy(
        src_ref=src, dst_ref=dst, send_sem=send_sem, recv_sem=recv_sem,
        device_id={"cell": cell, "rank": rank}, device_id_type=MESH)


def unless(flag):
    return pl.when(jnp.logical_not(flag))


def kernel(tri, w, fac_hbm, tgt, out, fac, msg, amsg, col, acol, bfull, cfull, wa, tg, scaled, pm_own, pm_send, pm_recv,
           resid, resid_t, ga, gb, gc, gb_send, gc_send, b1, c1, b2_send, c2_send, b2, c2, asend, arecv,
           l_sem, t_sem, col_s, col_r, acol_s, acol_r, g_s, g_r, pm_s, pm_r, r_s, r_r, f_s, f_r, a_s, a_r):
    cell = lax.axis_index("cell")
    zh = lax.axis_index("rank")
    core = cell % 2
    zl = (cell // 2) % 2
    y = (cell // 4) % 4
    x = cell // 16
    rows = w.shape[1]
    hw = rows // 2
    me = cell_of(x, y, zl, core)
    other = cell_of(x, y, zl, 1 - core)

    load = pltpu.make_async_copy(fac_hbm, fac, l_sem.at[0])
    load.start()
    own_tgt = pltpu.make_async_copy(tgt.at[zh], tg.at[pl.ds(core * 4, 4)], l_sem.at[1])
    own_tgt.start()

    barrier = pltpu.get_barrier_semaphore()

    def greet(to, rank):
        pl.semaphore_signal(barrier, inc=1, device_id={"cell": to, "rank": rank}, device_id_type=MESH)

    for s in range(4):
        @unless((zl == s // 2) & (core == s % 2) & (zh == core))
        def _():
            greet(cell_of(x, y, s // 2, s % 2), core)

    @pl.when(zh != core)
    def _():
        greet(other, zh)
    for d in range(1, 4):
        greet(cell_of((x + d) % 4, y, zl, core), zh)
        greet(cell_of(x, (y + d) % 4, zl, core), zh)

    load.wait()
    for t in range(2):
        a = w[...] * fac[tri[t, 0]]
        b = fac[tri[t, 1]]
        c = fac[tri[t, 2]]
        hi = a.astype(bf16).astype(f32)
        lo = a - hi
        msg[t] = jnp.concatenate([b[:, :hw], c[:, :hw], b[:, hw:], c[:, hw:]], axis=0).astype(bf16)
        amsg[t] = jnp.concatenate([hi[:, :hw], lo[:, :hw], hi[:, hw:], lo[:, hw:]], axis=0).astype(bf16)
    pl.semaphore_wait(barrier, 10)

    slot = zl * 2 + core

    def col_copy(t, dl):
        return rcopy(msg.at[t], col.at[slot], col_s.at[t * 2 + dl], col_r.at[slot], cell_of(x, y, (zl + dl) % 2, zh), t)

    def acol_copy(t):
        return rcopy(amsg.at[t], acol.at[core], acol_s.at[t], acol_r.at[core], cell_of(x, y, zl, zh), t)

    for dl in (1, 0):
        for t in range(2):
            if dl == 1:
                col_copy(t, dl).start()
            else:
                is_self = (core == zh) & (zh == t)

                @unless(is_self)
                def _():
                    col_copy(t, dl).start()
                    acol_copy(t).start()

                @pl.when(is_self)
                def _():
                    col[slot] = msg[t]
                    acol[core] = amsg[t]
    for s in range(4):
        @unless((core == zh) & (slot == s))
        def _():
            rcopy(msg.at[0], col.at[s], col_s.at[0], col_r.at[s], other, zh).wait_recv()
    got = [col[s].astype(f32) for s in range(4)]
    for h in range(2):
        bfull[h, x, y] = jnp.concatenate([m[8 * h:8 * h + 4] for m in got], axis=0).astype(bf16)
        cfull[h, x, y] = jnp.concatenate([m[8 * h + 4:8 * h + 8] for m in got], axis=0).astype(bf16)

    first_pos, second_pos = (x, y), (y, x)

    def block(which, h, p, q):
        return bfull.at[h, p, q] if which == 0 else cfull.at[h, q, p]

    def along_first(which, d):
        return cell_of((x + d) % 4, y, zl, core) if which == 0 else cell_of(x, (y + d) % 4, zl, core)

    def along_second(which, d):
        return along_first(1 - which, d)

    def gather_copy(which, h, p, q, k, to):
        view = block(which, h, p % 4, q % 4)
        n = (which * 2 + h) * 16 + k
        return rcopy(view, view, g_s.at[n], g_r.at[n], to, zh)

    gathers = []

    def send(*args):
        gathers.append(gather_copy(*args))
        gathers[-1].start()

    def first(which, h, d):
        send(which, h, first_pos[which], second_pos[which], d, along_first(which, d))

    def first_wait(which, h, d):
        gather_copy(which, h, first_pos[which] + 4 - d, second_pos[which], d, other).wait_recv()

    def near(which, h, e):
        for up in (1, 0):
            send(which, h, first_pos[which] + e, second_pos[which], 4 + 2 * e + up, along_second(which, 1 if up else 3))

    def near_wait(which, h, e, up):
        gather_copy(which, h, first_pos[which] + e, second_pos[which] + (3 if up else 1), 4 + 2 * e + up, other).wait_recv()

    def forward(which, h, e):
        up = 1 if e in (0, 2) else 0
        near_wait(which, h, e, up)
        send(which, h, first_pos[which] + e, second_pos[which] + (3 if up else 1), 12 + e, along_second(which, 1 if up else 3))

    def far_wait(which, h, e):
        gather_copy(which, h, first_pos[which] + e, second_pos[which] + 2, 12 + e, other).wait_recv()

    both = [(which, h) for h in range(2) for which in range(2)]
    for d in (2, 1, 3):
        for which, h in both:
            first(which, h, d)
    for which, h in both:
        near(which, h, 0)

    tg_copy = rcopy(tgt.at[zh], tg.at[pl.ds(core * 4, 4)], t_sem.at[0], t_sem.at[1], other, zh)
    tg_copy.start()
    for c in range(2):
        @unless((core == zh) & (core == c))
        def _():
            rcopy(amsg.at[0], acol.at[c], acol_s.at[0], acol_r.at[c], other, zh).wait_recv()
    got = [acol[c].astype(f32) for c in range(2)]
    for h in range(2):
        wa[:, h * hw:(h + 1) * hw] = jnp.concatenate([m[8 * h:8 * h + 4] + m[8 * h + 4:8 * h + 8] for m in got], axis=0)

    for d in (1, 3):
        for which, h in both:
            first_wait(which, h, d)
            near(which, h, 4 - d)
    for which, h in both:
        first_wait(which, h, 2)
        near(which, h, 2)
    for e in (0, 1, 3, 2):
        for which, h in both:
            forward(which, h, e)

    def pm_copy(i):
        return rcopy(pm_send.at[i], pm_recv.at[i], pm_s.at[i], pm_r.at[i], other, zh)

    for h in range(2):
        for which in range(2):
            for e, up in ((0, 0), (1, 1), (3, 1), (2, 0)):
                near_wait(which, h, e, up)
        for e in (0, 1, 3, 2):
            for which in range(2):
                far_wait(which, h, e)

        @pl.loop(0, 8)
        def _(i):
            wrow = wa[pl.ds(i, 1), h * hw:(h + 1) * hw]
            s = (wrow * bfull[h].reshape(256, hw).astype(f32)).astype(bf16)
            scaled[h, pl.ds(pl.multiple_of(i * 256, 256), 256), :] = s
            pm = lax.dot_general(s, cfull[h].reshape(256, hw), NT, preferred_element_type=f32)
            if h == 0:
                pm_own[i] = pm
            else:
                pm = pm_own[i] + pm
                pm_own[i] = pm
                pm_send[i] = pm.astype(bf16)
                pm_copy(i).start()

    own_tgt.wait()
    rcopy(tgt.at[zh], tg.at[pl.ds((1 - core) * 4, 4)], t_sem.at[0], t_sem.at[1], other, zh).wait_recv()

    @pl.loop(0, 8)
    def _(i):
        pm_copy(i).wait_recv()
        r = (pm_own[i] + pm_recv[i].astype(f32) - tg[i].astype(f32)).astype(bf16)
        at = pl.multiple_of(i * 256, 256)
        resid[pl.ds(at, 256), :] = r
        resid_t[:, pl.ds(at, 256)] = r.T

    scatters = []

    def scatter(src, dst, which, h, d, to):
        n = (which * 2 + h) * 4 + d
        scatters.append(rcopy(src, dst, r_s.at[n], r_r.at[n], to, zh))
        scatters[-1].start()

    def scatter_wait(which, h, d):
        n = (which * 2 + h) * 4 + d
        dst = (b1, c1)[which].at[h, d - 1]
        rcopy(dst, dst, r_s.at[n], r_r.at[n], other, zh).wait_recv()

    for h in range(2):
        part = jnp.dot(resid_t[...], scaled[h], preferred_element_type=f32)
        gc[h] = part.reshape(4, 4, 16, hw)
        gc_send[h] = part.reshape(4, 4, 16, hw).astype(bf16)
        for d in (2, 1, 3):
            scatter(gc_send.at[h, (x + d) % 4], c1.at[h, d - 1], 1, h, d, cell_of((x + d) % 4, y, zl, core))

        @pl.loop(0, 2)
        def _(q):
            lanes = pl.ds(pl.multiple_of(q * 256, 256), 256)
            wlanes = pl.ds(pl.multiple_of(h * hw + q * 256, 256), 256)
            cs = cfull[h, :, :, :, lanes].reshape(256, 256)
            bs = bfull[h, :, :, :, lanes].reshape(256, 256).astype(f32)
            acc = jnp.zeros((256, 256), f32)
            for i in range(8):
                xprod = jnp.dot(resid[i * 256:(i + 1) * 256, :], cs, preferred_element_type=f32)
                ga[i:i + 1, wlanes] = jnp.sum(xprod * bs, axis=0, keepdims=True)
                acc = acc + wa[i:i + 1, wlanes] * xprod
            gb[h, :, :, :, lanes] = acc.reshape(4, 4, 16, 256)
            gb_send[h, :, :, :, lanes] = acc.reshape(4, 4, 16, 256).astype(bf16)
        for d in (2, 1, 3):
            scatter(gb_send.at[h, :, (y + d) % 4], b1.at[h, d - 1], 0, h, d, cell_of(x, (y + d) % 4, zl, core))

    def a_copy(c):
        return rcopy(asend.at[c], arecv.at[zh], a_s.at[c], a_r.at[zh], cell_of(x, y, zl, c), core)

    for c in range(2):
        asend[c] = jnp.concatenate([ga[4 * c:4 * c + 4, :hw], ga[4 * c:4 * c + 4, hw:]], axis=0)
        is_self = (core == c) & (zh == core)

        @unless(is_self)
        def _():
            a_copy(c).start()

        @pl.when(is_self)
        def _():
            arecv[zh] = asend[c]

    def final_copy(which, h, d, s, to_wait=False):
        buf_s, buf_r = ((b2_send, b2), (c2_send, c2))[which]
        p = first_pos[which]
        n = (which * 2 + h) * 16
        if which == 0:
            to = cell_of((x + d) % 4, y, s // 2, s % 2)
        else:
            to = cell_of(x, (y + d) % 4, s // 2, s % 2)
        at = (p * 2 + zl) * 2 + zh
        return rcopy(buf_s.at[h, (p + d) % 4, s], buf_r.at[h, at], f_s.at[n + d * 4 + s], f_r.at[n + at], to, core)

    def final_self(d, s):
        return (zl == s // 2) & (core == s % 2) & (zh == core) if d == 0 else None

    order = [(1, 0), (0, 0), (1, 1), (0, 1)]
    for which, h in order:
        for d in (1, 3, 2):
            scatter_wait(which, h, d)
        if which == 0:
            total = gb[h, :, y] + b1[h, 0].astype(f32) + b1[h, 1].astype(f32) + b1[h, 2].astype(f32)
        else:
            total = gc[h, x] + c1[h, 0].astype(f32) + c1[h, 1].astype(f32) + c1[h, 2].astype(f32)
        buf_s, buf_r = ((b2_send, b2), (c2_send, c2))[which]
        for p in range(4):
            for s in range(4):
                buf_s[h, p, s] = jnp.concatenate(
                    [total[p, 4 * s:4 * s + 4, 128 * q:128 * q + 128] for q in range(4)], axis=0).astype(bf16)
        for d in (2, 1, 3, 0):
            for s in range(4):
                if d:
                    final_copy(which, h, d, s).start()
                else:
                    @unless(final_self(d, s))
                    def _():
                        final_copy(which, h, d, s).start()

                    @pl.when(final_self(d, s))
                    def _():
                        buf_r[h, (first_pos[which] * 2 + zl) * 2 + zh] = buf_s[h, first_pos[which], s]

    for c in range(2):
        @unless((c == zh) & (zh == core))
        def _():
            rcopy(asend.at[0], arecv.at[c], a_s.at[0], a_r.at[c], other, zh).wait_recv()
    sums = {}
    for which, h in order:
        buf_r = (b2, c2)[which]
        for d in (0, 1, 3, 2):
            for k in range(4):
                at = ((first_pos[which] + d) % 4) * 4 + k
                n = (which * 2 + h) * 16 + at
                take = rcopy(buf_r.at[h, at], buf_r.at[h, at], f_s.at[0], f_r.at[n], other, zh)
                if d:
                    take.wait_recv()
                else:
                    @unless((zl == k // 2) & (zh == k % 2) & (zh == core))
                    def _():
                        take.wait_recv()
        for t in range(2):
            total = sum(buf_r[h, 2 * k + t].astype(f32) for k in range(8))
            sums[which, h, t] = jnp.concatenate([total[4 * q:4 * q + 4] for q in range(4)], axis=1)
    steps = []
    for t in range(2):
        g = arecv[t]
        steps.append((tri[t, 0], learn_rate * (w[...] * jnp.concatenate([g[0:4], g[4:8]], axis=1))))
        for which in range(2):
            g = jnp.concatenate([sums[which, 0, t], sums[which, 1, t]], axis=1)
            steps.append((tri[t, 1 + which], learn_rate * g))

    @pl.loop(0, 48)
    def _(attr):
        step = jnp.zeros((4, rows), f32)
        for which, g in steps:
            step = step + jnp.where(which == attr, g, 0.0)
        out[attr] = fac[attr] - step

    for t in range(2):
        col_copy(t, 1).wait_send()

        @unless((core == zh) & (zh == t))
        def _():
            col_copy(t, 0).wait_send()
            acol_copy(t).wait_send()
    tg_copy.wait_send()
    for copy in gathers + scatters:
        copy.wait_send()

    @pl.loop(0, 8)
    def _(i):
        pm_copy(i).wait_send()
    for c in range(2):
        @unless((core == c) & (zh == core))
        def _():
            a_copy(c).wait_send()
    for which, h in order:
        for d in range(4):
            for s in range(4):
                if d:
                    final_copy(which, h, d, s).wait_send()
                else:
                    @unless(final_self(d, s))
                    def _():
                        final_copy(which, h, d, s).wait_send()


def on_device(factors, rank_weights, triples, targets):
    rows = rank_weights.shape[0]
    hw = rows // 2
    vmem = pl.BlockSpec(memory_space=pltpu.VMEM)
    hbm = pl.BlockSpec(memory_space=pl.ANY)
    dma = pltpu.SemaphoreType.DMA
    V = pltpu.VMEM
    return pl.pallas_call(
        kernel,
        out_shape=jax.ShapeDtypeStruct(factors.shape, f32),
        in_specs=[pl.BlockSpec(memory_space=pltpu.SMEM), vmem, hbm, hbm],
        out_specs=vmem,
        scratch_shapes=[
            V(factors.shape, f32),
            V((2, 16, hw), bf16),
            V((2, 16, hw), bf16),
            V((4, 16, hw), bf16),
            V((2, 16, hw), bf16),
            V((2, 4, 4, 16, hw), bf16),
            V((2, 4, 4, 16, hw), bf16),
            V((8, rows), f32),
            V((8, 256, 256), bf16),
            V((2, 2048, hw), bf16),
            V((8, 256, 256), f32),
            V((8, 256, 256), bf16),
            V((8, 256, 256), bf16),
            V((2048, 256), bf16),
            V((256, 2048), bf16),
            V((8, rows), f32),
            V((2, 4, 4, 16, hw), f32),
            V((2, 4, 4, 16, hw), f32),
            V((2, 4, 4, 16, hw), bf16),
            V((2, 4, 4, 16, hw), bf16),
            V((2, 3, 4, 16, hw), bf16),
            V((2, 3, 4, 16, hw), bf16),
            V((2, 4, 4, 16, 128), bf16),
            V((2, 4, 4, 16, 128), bf16),
            V((2, 16, 16, 128), bf16),
            V((2, 16, 16, 128), bf16),
            V((2, 8, hw), f32),
            V((2, 8, hw), f32),
            dma((2,)), dma((2,)), dma((4,)), dma((4,)), dma((2,)), dma((2,)), dma((64,)), dma((64,)),
            dma((8,)), dma((8,)), dma((16,)), dma((16,)), dma((64,)), dma((64,)), dma((2,)), dma((2,)),
        ],
        compiler_params=pltpu.CompilerParams(collective_id=0, has_side_effects=True, vmem_limit_bytes=56 * 1024 * 1024),
    )(triples, rank_weights.reshape(1, rows), factors, targets)


def solution(mesh):
    in_specs = (P(None, "cell", "rank"), P("rank"), P(), P(None, "cell", None, None))
    return jax.shard_map(on_device, mesh=mesh, in_specs=in_specs, out_specs=P(None, "cell", "rank"), check_vma=False)
```

```python
import jax
import jax.numpy as jnp
from jax import lax
from jax.experimental import pallas as pl
from jax.experimental.pallas import tpu as pltpu
from jax.sharding import PartitionSpec as P

learn_rate = 0.02
MESH = pl.DeviceIdType.MESH
f32, bf16 = jnp.float32, jnp.bfloat16
NT = (((1,), (1,)), ((), ()))


def cell_of(x, y, zl, core):
    return ((x * 4 + y) * 2 + zl) * 2 + core


def rcopy(src, dst, send_sem, recv_sem, cell, rank):
    return pltpu.make_async_remote_copy(
        src_ref=src, dst_ref=dst, send_sem=send_sem, recv_sem=recv_sem,
        device_id={"cell": cell, "rank": rank}, device_id_type=MESH)


def arrived(ref, sem):
    rcopy(ref, ref, sem, sem, 0, 0).wait_recv()


def unless(flag):
    return pl.when(jnp.logical_not(flag))


def kernel(tri, w, fac_hbm, tgt, out, fac, msg, amsg, col, acol, bfull, cfull, wa, tg, scaled, pm_own, pm_send, pm_recv,
           resid, resid_t, ga, gb, gc, gb_send, gc_send, b1, c1, b2_send, c2_send, b2, c2, asend, arecv,
           l_sem, t_sem, sent, col_r, first_r, near_r, far_r, pm_r, r_r, f_r):
    cell = lax.axis_index("cell")
    zh = lax.axis_index("rank")
    core = cell % 2
    zl = (cell // 2) % 2
    y = (cell // 4) % 4
    x = cell // 16
    rows = w.shape[1]
    hw = rows // 2
    me = cell_of(x, y, zl, core)
    other = cell_of(x, y, zl, 1 - core)

    load = pltpu.make_async_copy(fac_hbm, fac, l_sem.at[0])
    load.start()
    own_tgt = pltpu.make_async_copy(tgt.at[zh], tg.at[pl.ds(core * 4, 4)], l_sem.at[1])
    own_tgt.start()

    barrier = pltpu.get_barrier_semaphore()

    def greet(to, rank):
        pl.semaphore_signal(barrier, inc=1, device_id={"cell": to, "rank": rank}, device_id_type=MESH)

    for s in range(4):
        @unless((zl == s // 2) & (core == s % 2) & (zh == core))
        def _():
            greet(cell_of(x, y, s // 2, s % 2), core)

    @pl.when(zh != core)
    def _():
        greet(other, zh)
    for d in range(1, 4):
        greet(cell_of((x + d) % 4, y, zl, core), zh)
        greet(cell_of(x, (y + d) % 4, zl, core), zh)

    load.wait()
    for t in range(2):
        a = w[...] * fac[tri[t, 0]]
        b = fac[tri[t, 1]]
        c = fac[tri[t, 2]]
        hi = a.astype(bf16).astype(f32)
        lo = a - hi
        msg[t] = jnp.concatenate([b[:, :hw], c[:, :hw], b[:, hw:], c[:, hw:]], axis=0).astype(bf16)
        amsg[t] = jnp.concatenate([hi[:, :hw], lo[:, :hw], hi[:, hw:], lo[:, hw:]], axis=0).astype(bf16)
    pl.semaphore_wait(barrier, 10)

    slot = zl * 2 + core

    def col_copy(t, dl):
        return rcopy(msg.at[t], col.at[slot], sent.at[0], col_r.at[0], cell_of(x, y, (zl + dl) % 2, zh), t)

    def acol_copy(t):
        return rcopy(amsg.at[t], acol.at[core], sent.at[0], col_r.at[1], cell_of(x, y, zl, zh), t)

    for dl in (1, 0):
        for t in range(2):
            if dl == 1:
                col_copy(t, dl).start()
            else:
                is_self = (core == zh) & (zh == t)

                @unless(is_self)
                def _():
                    col_copy(t, dl).start()
                    acol_copy(t).start()

                @pl.when(is_self)
                def _():
                    col[slot] = msg[t]
                    acol[core] = amsg[t]

    @unless(core == zh)
    def _():
        arrived(col, col_r.at[0])

    @pl.when(core == zh)
    def _():
        arrived(col.at[pl.ds(0, 3)], col_r.at[0])

    got = [col[s].astype(f32) for s in range(4)]
    for h in range(2):
        bfull[h, x, y] = jnp.concatenate([m[8 * h:8 * h + 4] for m in got], axis=0).astype(bf16)
        cfull[h, x, y] = jnp.concatenate([m[8 * h + 4:8 * h + 8] for m in got], axis=0).astype(bf16)

    first_pos, second_pos = (x, y), (y, x)

    def block(which, h, p, q):
        return bfull.at[h, p, q] if which == 0 else cfull.at[h, q, p]

    def along_first(which, d):
        return cell_of((x + d) % 4, y, zl, core) if which == 0 else cell_of(x, (y + d) % 4, zl, core)

    def along_second(which, d):
        return along_first(1 - which, d)

    def send(which, h, p, q, recv_sem, to):
        view = block(which, h, p % 4, q % 4)
        rcopy(view, view, sent.at[1], recv_sem, to, zh).start()

    def first(which, d):
        view = block(which, slice(None), first_pos[which], second_pos[which])
        rcopy(view, view, sent.at[1], first_r.at[which * 3 + d - 1], along_first(which, d), zh).start()

    def first_wait(which, d):
        arrived(block(which, slice(None), (first_pos[which] + 4 - d) % 4, second_pos[which]), first_r.at[which * 3 + d - 1])

    passed_on = {1: (0, 2), 0: (1, 3)}

    def near_sem(which, h, e, up):
        return near_r.at[(which * 2 + h) * 5 + (e if e in passed_on[up] else 4)]

    def near(which, h, e):
        for up in (1, 0):
            send(which, h, first_pos[which] + e, second_pos[which], near_sem(which, h, e, up), along_second(which, 1 if up else 3))

    def forward(which, h, e):
        up = 1 if e in passed_on[1] else 0
        p, q = first_pos[which] + e, second_pos[which] + (3 if up else 1)
        arrived(block(which, h, p % 4, q % 4), near_sem(which, h, e, up))
        send(which, h, p, q, far_r.at[which * 2 + h], along_second(which, 1 if up else 3))

    both = [(which, h) for h in range(2) for which in range(2)]
    for d in (2, 1, 3):
        for which in range(2):
            first(which, d)
    for which, h in both:
        near(which, h, 0)

    tg_copy = rcopy(tgt.at[zh], tg.at[pl.ds(core * 4, 4)], t_sem.at[0], t_sem.at[1], other, zh)
    tg_copy.start()

    @unless(core == zh)
    def _():
        arrived(acol, col_r.at[1])

    @pl.when(core == zh)
    def _():
        arrived(acol.at[0], col_r.at[1])

    got = [acol[c].astype(f32) for c in range(2)]
    for h in range(2):
        wa[:, h * hw:(h + 1) * hw] = jnp.concatenate([m[8 * h:8 * h + 4] + m[8 * h + 4:8 * h + 8] for m in got], axis=0)

    for d in (1, 3, 2):
        for which in range(2):
            first_wait(which, d)
            near(which, 0, 4 - d)
            near(which, 1, 4 - d)
    for e in (0, 1, 3, 2):
        for which, h in both:
            forward(which, h, e)

    def pm_copy(i):
        part = pl.ds(i, 2)
        return rcopy(pm_send.at[part], pm_recv.at[part], sent.at[2], pm_r.at[i // 2], other, zh)

    for h in range(2):
        for which in range(2):
            arrived(bfull.at[h, 0], near_r.at[(which * 2 + h) * 5 + 4])
            arrived(bfull.at[h, 0], far_r.at[which * 2 + h])
        bs = bfull[h].reshape(256, hw).astype(f32)
        cs = cfull[h].reshape(256, hw)
        for i in range(8):
            s = (wa[i:i + 1, h * hw:(h + 1) * hw] * bs).astype(bf16)
            scaled[h, i * 256:(i + 1) * 256, :] = s
            pm = lax.dot_general(s, cs, NT, preferred_element_type=f32)
            if h == 0:
                pm_own[i] = pm
            else:
                pm = pm_own[i] + pm
                pm_own[i] = pm
                pm_send[i] = pm.astype(bf16)
                if i % 2:
                    pm_copy(i - 1).start()

    own_tgt.wait()
    arrived(tg.at[pl.ds((1 - core) * 4, 4)], t_sem.at[1])

    for i in range(8):
        if i % 2 == 0:
            arrived(pm_recv.at[pl.ds(i, 2)], pm_r.at[i // 2])
        r = (pm_own[i] + pm_recv[i].astype(f32) - tg[i].astype(f32)).astype(bf16)
        resid[i * 256:(i + 1) * 256, :] = r
        resid_t[:, i * 256:(i + 1) * 256] = r.T

    def scatter(src, dst, which, h, to):
        rcopy(src, dst, sent.at[3], r_r.at[which * 2 + h], to, zh).start()

    for h in range(2):
        for q in range(2):
            lanes = slice(q * 256, (q + 1) * 256)
            wlanes = slice(h * hw + q * 256, h * hw + (q + 1) * 256)
            part = jnp.dot(resid_t[...], scaled[h, :, lanes], preferred_element_type=f32).reshape(4, 4, 16, 256)
            gc[h, q] = part
            gc_send[h, q] = part.astype(bf16)
            for d in (2, 1, 3):
                scatter(gc_send.at[h, q, (x + d) % 4], c1.at[h, d - 1, q], 1, h, cell_of((x + d) % 4, y, zl, core))
            cs = cfull[h, :, :, :, lanes].reshape(256, 256)
            bs = bfull[h, :, :, :, lanes].reshape(256, 256).astype(f32)
            acc = jnp.zeros((256, 256), f32)
            for i in range(8):
                xprod = jnp.dot(resid[i * 256:(i + 1) * 256, :], cs, preferred_element_type=f32)
                ga[i:i + 1, wlanes] = jnp.sum(xprod * bs, axis=0, keepdims=True)
                acc = acc + wa[i:i + 1, wlanes] * xprod
            acc = acc.reshape(4, 4, 16, 256)
            gb[h, q] = acc
            gb_send[h, q] = acc.astype(bf16)
            for d in (2, 1, 3):
                scatter(gb_send.at[h, q, :, (y + d) % 4], b1.at[h, d - 1, q], 0, h, cell_of(x, (y + d) % 4, zl, core))

    def a_copy(c):
        return rcopy(asend.at[c], arecv.at[zh], sent.at[4], col_r.at[2], cell_of(x, y, zl, c), core)

    for c in range(2):
        asend[c] = jnp.concatenate([ga[4 * c:4 * c + 4, :hw], ga[4 * c:4 * c + 4, hw:]], axis=0)
        is_self = (core == c) & (zh == core)

        @unless(is_self)
        def _():
            a_copy(c).start()

        @pl.when(is_self)
        def _():
            arecv[zh] = asend[c]

    def final_copy(which, h, d, s):
        buf_s, buf_r = ((b2_send, b2), (c2_send, c2))[which]
        p = first_pos[which]
        if which == 0:
            to = cell_of((x + d) % 4, y, s // 2, s % 2)
        else:
            to = cell_of(x, (y + d) % 4, s // 2, s % 2)
        at = (p * 2 + zl) * 2 + zh
        return rcopy(buf_s.at[h, (p + d) % 4, s], buf_r.at[h, at], sent.at[5], f_r.at[which * 2 + h], to, core)

    def final_self(d, s):
        return (zl == s // 2) & (core == s % 2) & (zh == core) if d == 0 else None

    order = [(1, 0), (0, 0), (1, 1), (0, 1)]
    for which, h in order:
        buf, mine = (b1, gb[h, :, :, y]) if which == 0 else (c1, gc[h, :, x])
        arrived(buf.at[h], r_r.at[which * 2 + h])
        total = mine + buf[h, 0].astype(f32) + buf[h, 1].astype(f32) + buf[h, 2].astype(f32)
        buf_s, buf_r = ((b2_send, b2), (c2_send, c2))[which]
        for p in range(4):
            for s in range(4):
                buf_s[h, p, s] = jnp.concatenate(
                    [total[q // 2, p, 4 * s:4 * s + 4, 128 * (q % 2):128 * (q % 2) + 128] for q in range(4)], axis=0).astype(bf16)
        for d in (2, 1, 3, 0):
            for s in range(4):
                if d:
                    final_copy(which, h, d, s).start()
                else:
                    @unless(final_self(d, s))
                    def _():
                        final_copy(which, h, d, s).start()

                    @pl.when(final_self(d, s))
                    def _():
                        buf_r[h, (first_pos[which] * 2 + zl) * 2 + zh] = buf_s[h, first_pos[which], s]

    @unless(zh == core)
    def _():
        arrived(arecv, col_r.at[2])

    @pl.when(zh == core)
    def _():
        arrived(arecv.at[0], col_r.at[2])

    sums = {}
    for which, h in order:
        buf_r = (b2, c2)[which]

        @unless(zh == core)
        def _():
            arrived(buf_r.at[h], f_r.at[which * 2 + h])

        @pl.when(zh == core)
        def _():
            arrived(buf_r.at[h, pl.ds(0, 15)], f_r.at[which * 2 + h])

        for t in range(2):
            total = sum(buf_r[h, 2 * k + t].astype(f32) for k in range(8))
            sums[which, h, t] = jnp.concatenate([total[4 * q:4 * q + 4] for q in range(4)], axis=1)
    steps = []
    for t in range(2):
        g = arecv[t]
        steps.append((tri[t, 0], learn_rate * (w[...] * jnp.concatenate([g[0:4], g[4:8]], axis=1))))
        for which in range(2):
            g = jnp.concatenate([sums[which, 0, t], sums[which, 1, t]], axis=1)
            steps.append((tri[t, 1 + which], learn_rate * g))

    @pl.loop(0, 48)
    def _(attr):
        step = jnp.zeros((4, rows), f32)
        for which, g in steps:
            step = step + jnp.where(which == attr, g, 0.0)
        out[attr] = fac[attr] - step

    def left(ref, k):
        rcopy(ref, ref, sent.at[k], sent.at[k], 0, 0).wait_send()

    tg_copy.wait_send()
    left(scaled.at[0, pl.ds(0, 960)], 1)
    left(pm_send, 2)
    left(scaled.at[0, pl.ds(0, 768)], 3)

    @unless(zh == core)
    def _():
        left(scaled.at[0, pl.ds(0, 96)], 0)
        left(asend, 4)
        left(scaled.at[0, pl.ds(0, 256)], 5)

    @pl.when(zh == core)
    def _():
        left(scaled.at[0, pl.ds(0, 64)], 0)
        left(asend.at[0], 4)
        left(scaled.at[0, pl.ds(0, 240)], 5)


def on_device(factors, rank_weights, triples, targets):
    rows = rank_weights.shape[0]
    hw = rows // 2
    vmem = pl.BlockSpec(memory_space=pltpu.VMEM)
    hbm = pl.BlockSpec(memory_space=pl.ANY)
    dma = pltpu.SemaphoreType.DMA
    V = pltpu.VMEM
    return pl.pallas_call(
        kernel,
        out_shape=jax.ShapeDtypeStruct(factors.shape, f32),
        in_specs=[pl.BlockSpec(memory_space=pltpu.SMEM), vmem, hbm, hbm],
        out_specs=vmem,
        scratch_shapes=[
            V(factors.shape, f32),
            V((2, 16, hw), bf16),
            V((2, 16, hw), bf16),
            V((4, 16, hw), bf16),
            V((2, 16, hw), bf16),
            V((2, 4, 4, 16, hw), bf16),
            V((2, 4, 4, 16, hw), bf16),
            V((8, rows), f32),
            V((8, 256, 256), bf16),
            V((2, 2048, hw), bf16),
            V((8, 256, 256), f32),
            V((8, 256, 256), bf16),
            V((8, 256, 256), bf16),
            V((2048, 256), bf16),
            V((256, 2048), bf16),
            V((8, rows), f32),
            V((2, 2, 4, 4, 16, 256), f32),
            V((2, 2, 4, 4, 16, 256), f32),
            V((2, 2, 4, 4, 16, 256), bf16),
            V((2, 2, 4, 4, 16, 256), bf16),
            V((2, 3, 2, 4, 16, 256), bf16),
            V((2, 3, 2, 4, 16, 256), bf16),
            V((2, 4, 4, 16, 128), bf16),
            V((2, 4, 4, 16, 128), bf16),
            V((2, 16, 16, 128), bf16),
            V((2, 16, 16, 128), bf16),
            V((2, 8, hw), f32),
            V((2, 8, hw), f32),
            dma((2,)), dma((2,)), dma((6,)), dma((3,)), dma((6,)), dma((20,)), dma((4,)), dma((4,)), dma((4,)), dma((4,)),
        ],
        compiler_params=pltpu.CompilerParams(collective_id=0, has_side_effects=True, vmem_limit_bytes=56 * 1024 * 1024),
    )(triples, rank_weights.reshape(1, rows), factors, targets)


def solution(mesh):
    in_specs = (P(None, "cell", "rank"), P("rank"), P(), P(None, "cell", None, None))
    return jax.shard_map(on_device, mesh=mesh, in_specs=in_specs, out_specs=P(None, "cell", "rank"), check_vma=False)
```

```python
import jax
import jax.numpy as jnp
from jax import lax
from jax.experimental import pallas as pl
from jax.experimental.pallas import tpu as pltpu
from jax.sharding import PartitionSpec as P

learn_rate = 0.02
MESH = pl.DeviceIdType.MESH
f32, bf16 = jnp.float32, jnp.bfloat16
NT = (((1,), (1,)), ((), ()))


def cell_of(x, y, zl, core):
    return ((x * 4 + y) * 2 + zl) * 2 + core


def rcopy(src, dst, send_sem, recv_sem, cell, rank):
    return pltpu.make_async_remote_copy(
        src_ref=src, dst_ref=dst, send_sem=send_sem, recv_sem=recv_sem,
        device_id={"cell": cell, "rank": rank}, device_id_type=MESH)


def arrived(ref, sem):
    rcopy(ref, ref, sem, sem, 0, 0).wait_recv()


def unless(flag):
    return pl.when(jnp.logical_not(flag))


def kernel(tri, w, fac_hbm, tgt, out, fac, msg, amsg, col, acol, bfull, cfull, wa, tg, scaled, pm_own, pm_send, pm_recv,
           resid, resid_t, ga, gb, gc, gb_send, gc_send, b1, c1, b2_send, c2_send, b2, c2, asend, arecv,
           l_sem, t_sem, sent, col_r, first_r, near_r, far_r, pm_r, r_r, f_r):
    cell = lax.axis_index("cell")
    zh = lax.axis_index("rank")
    core = cell % 2
    zl = (cell // 2) % 2
    y = (cell // 4) % 4
    x = cell // 16
    rows = w.shape[1]
    hw = rows // 2
    me = cell_of(x, y, zl, core)
    other = cell_of(x, y, zl, 1 - core)

    load = pltpu.make_async_copy(fac_hbm, fac, l_sem.at[0])
    load.start()
    own_tgt = pltpu.make_async_copy(tgt.at[zh], tg.at[pl.ds(core * 4, 4)], l_sem.at[1])
    own_tgt.start()

    barrier = pltpu.get_barrier_semaphore()

    def greet(to, rank):
        pl.semaphore_signal(barrier, inc=1, device_id={"cell": to, "rank": rank}, device_id_type=MESH)

    for s in range(4):
        @unless((zl == s // 2) & (core == s % 2) & (zh == core))
        def _():
            greet(cell_of(x, y, s // 2, s % 2), core)

    @pl.when(zh != core)
    def _():
        greet(other, zh)
    for d in range(1, 4):
        greet(cell_of((x + d) % 4, y, zl, core), zh)
        greet(cell_of(x, (y + d) % 4, zl, core), zh)

    load.wait()
    for t in range(2):
        a = w[...] * fac[tri[t, 0]]
        b = fac[tri[t, 1]]
        c = fac[tri[t, 2]]
        hi = a.astype(bf16).astype(f32)
        lo = a - hi
        msg[t] = jnp.concatenate([b[:, :hw], c[:, :hw], b[:, hw:], c[:, hw:]], axis=0).astype(bf16)
        amsg[t] = jnp.concatenate([hi[:, :hw], lo[:, :hw], hi[:, hw:], lo[:, hw:]], axis=0).astype(bf16)
    pl.semaphore_wait(barrier, 10)

    slot = zl * 2 + core

    def col_copy(t, dl):
        return rcopy(msg.at[t], col.at[slot], sent.at[0], col_r.at[0], cell_of(x, y, (zl + dl) % 2, zh), t)

    def acol_copy(t):
        return rcopy(amsg.at[t], acol.at[core], sent.at[0], col_r.at[1], cell_of(x, y, zl, zh), t)

    for dl in (1, 0):
        for t in range(2):
            if dl == 1:
                col_copy(t, dl).start()
            else:
                is_self = (core == zh) & (zh == t)

                @unless(is_self)
                def _():
                    col_copy(t, dl).start()
                    acol_copy(t).start()

                @pl.when(is_self)
                def _():
                    col[slot] = msg[t]
                    acol[core] = amsg[t]

    @unless(core == zh)
    def _():
        arrived(col, col_r.at[0])

    @pl.when(core == zh)
    def _():
        arrived(col.at[pl.ds(0, 3)], col_r.at[0])

    got = [col[s].astype(f32) for s in range(4)]
    for h in range(2):
        bfull[h, x, y] = jnp.concatenate([m[8 * h:8 * h + 4] for m in got], axis=0).astype(bf16)
        cfull[h, x, y] = jnp.concatenate([m[8 * h + 4:8 * h + 8] for m in got], axis=0).astype(bf16)

    first_pos, second_pos = (x, y), (y, x)

    def block(which, h, p, q):
        return bfull.at[h, p, q] if which == 0 else cfull.at[h, q, p]

    def along_first(which, d):
        return cell_of((x + d) % 4, y, zl, core) if which == 0 else cell_of(x, (y + d) % 4, zl, core)

    def along_second(which, d):
        return along_first(1 - which, d)

    def send(which, h, p, q, recv_sem, to):
        view = block(which, h, p % 4, q % 4)
        rcopy(view, view, sent.at[1], recv_sem, to, zh).start()

    def first(which, d):
        view = block(which, slice(None), first_pos[which], second_pos[which])
        rcopy(view, view, sent.at[1], first_r.at[which * 3 + d - 1], along_first(which, d), zh).start()

    def first_wait(which, d):
        arrived(block(which, slice(None), (first_pos[which] + 4 - d) % 4, second_pos[which]), first_r.at[which * 3 + d - 1])

    def passed_on(h, e, up):
        return (e, up) in (((0, 1), (1, 1), (3, 0)), ((0, 0), (1, 1), (3, 0)))[h]

    def near_sem(which, h, e, up):
        return near_r.at[(which * 2 + h) * 4 + ((0, 1, None, 2)[e] if passed_on(h, e, up) else 3)]

    def near(which, h, e):
        for up in (1, 0):
            send(which, h, first_pos[which] + e, second_pos[which], near_sem(which, h, e, up), along_second(which, 1 if up else 3))
        if e == 2:
            send(which, h, first_pos[which] + e, second_pos[which], far_r.at[which * 2 + h], along_second(which, 2))

    def forward(which, h, e):
        up = 1 if passed_on(h, e, 1) else 0
        p, q = first_pos[which] + e, second_pos[which] + (3 if up else 1)
        arrived(block(which, h, p % 4, q % 4), near_sem(which, h, e, up))
        send(which, h, p, q, far_r.at[which * 2 + h], along_second(which, 1 if up else 3))

    both = [(which, h) for h in range(2) for which in range(2)]
    for d in (2, 1, 3):
        for which in range(2):
            first(which, d)
    for which, h in both:
        near(which, h, 0)

    tg_copy = rcopy(tgt.at[zh], tg.at[pl.ds(core * 4, 4)], t_sem.at[0], t_sem.at[1], other, zh)
    tg_copy.start()

    @unless(core == zh)
    def _():
        arrived(acol, col_r.at[1])

    @pl.when(core == zh)
    def _():
        arrived(acol.at[0], col_r.at[1])

    got = [acol[c].astype(f32) for c in range(2)]
    for h in range(2):
        wa[:, h * hw:(h + 1) * hw] = jnp.concatenate([m[8 * h:8 * h + 4] + m[8 * h + 4:8 * h + 8] for m in got], axis=0)

    for d in (1, 3, 2):
        for which in range(2):
            first_wait(which, d)
            near(which, 0, 4 - d)
            near(which, 1, 4 - d)
    for e in (0, 1, 3):
        for which, h in both:
            forward(which, h, e)

    def pm_copy(i):
        part = pl.ds(i, 2)
        return rcopy(pm_send.at[part], pm_recv.at[part], sent.at[2], pm_r.at[i // 2], other, zh)

    five = scaled.at[0, pl.ds(0, 80)]
    for h in range(2):
        for which in range(2):
            arrived(five, near_r.at[(which * 2 + h) * 4 + 3])
            arrived(bfull.at[h, 0], far_r.at[which * 2 + h])
        bs = bfull[h].reshape(256, hw).astype(f32)
        cs = cfull[h].reshape(256, hw)
        for i in range(8):
            s = (wa[i:i + 1, h * hw:(h + 1) * hw] * bs).astype(bf16)
            scaled[h, i * 256:(i + 1) * 256, :] = s
            pm = lax.dot_general(s, cs, NT, preferred_element_type=f32)
            if h == 0:
                pm_own[i] = pm
            else:
                pm = pm_own[i] + pm
                pm_own[i] = pm
                pm_send[i] = pm.astype(bf16)
                if i % 2:
                    pm_copy(i - 1).start()

    own_tgt.wait()
    arrived(tg.at[pl.ds((1 - core) * 4, 4)], t_sem.at[1])

    for i in range(8):
        if i % 2 == 0:
            arrived(pm_recv.at[pl.ds(i, 2)], pm_r.at[i // 2])
        r = (pm_own[i] + pm_recv[i].astype(f32) - tg[i].astype(f32)).astype(bf16)
        resid[i * 256:(i + 1) * 256, :] = r
        resid_t[:, i * 256:(i + 1) * 256] = r.T

    def scatter(src, dst, which, h, to):
        rcopy(src, dst, sent.at[3], r_r.at[which * 2 + h], to, zh).start()

    for h in range(2):
        for q in range(2):
            lanes = slice(q * 256, (q + 1) * 256)
            wlanes = slice(h * hw + q * 256, h * hw + (q + 1) * 256)
            part = jnp.dot(resid_t[...], scaled[h, :, lanes], preferred_element_type=f32).reshape(4, 4, 16, 256)
            gc[h, q] = part
            gc_send[h, q] = part.astype(bf16)
            for d in (2, 1, 3):
                scatter(gc_send.at[h, q, (x + d) % 4], c1.at[h, d - 1, q], 1, h, cell_of((x + d) % 4, y, zl, core))
            cs = cfull[h, :, :, :, lanes].reshape(256, 256)
            bs = bfull[h, :, :, :, lanes].reshape(256, 256).astype(f32)
            acc = jnp.zeros((256, 256), f32)
            for i in range(8):
                xprod = jnp.dot(resid[i * 256:(i + 1) * 256, :], cs, preferred_element_type=f32)
                ga[i:i + 1, wlanes] = jnp.sum(xprod * bs, axis=0, keepdims=True)
                acc = acc + wa[i:i + 1, wlanes] * xprod
            acc = acc.reshape(4, 4, 16, 256)
            gb[h, q] = acc
            gb_send[h, q] = acc.astype(bf16)
            for d in (2, 1, 3):
                scatter(gb_send.at[h, q, :, (y + d) % 4], b1.at[h, d - 1, q], 0, h, cell_of(x, (y + d) % 4, zl, core))

    def a_copy(c):
        return rcopy(asend.at[c], arecv.at[zh], sent.at[4], col_r.at[2], cell_of(x, y, zl, c), core)

    for c in range(2):
        asend[c] = jnp.concatenate([ga[4 * c:4 * c + 4, :hw], ga[4 * c:4 * c + 4, hw:]], axis=0)
        is_self = (core == c) & (zh == core)

        @unless(is_self)
        def _():
            a_copy(c).start()

        @pl.when(is_self)
        def _():
            arecv[zh] = asend[c]

    def final_copy(which, h, d, s):
        buf_s, buf_r = ((b2_send, b2), (c2_send, c2))[which]
        p = first_pos[which]
        if which == 0:
            to = cell_of((x + d) % 4, y, s // 2, s % 2)
        else:
            to = cell_of(x, (y + d) % 4, s // 2, s % 2)
        at = (p * 2 + zl) * 2 + zh
        return rcopy(buf_s.at[h, (p + d) % 4, s], buf_r.at[h, at], sent.at[5], f_r.at[which * 2 + h], to, core)

    def final_self(d, s):
        return (zl == s // 2) & (core == s % 2) & (zh == core) if d == 0 else None

    order = [(1, 0), (0, 0), (1, 1), (0, 1)]
    for which, h in order:
        buf, mine = (b1, gb[h, :, :, y]) if which == 0 else (c1, gc[h, :, x])
        arrived(buf.at[h], r_r.at[which * 2 + h])
        total = mine + buf[h, 0].astype(f32) + buf[h, 1].astype(f32) + buf[h, 2].astype(f32)
        buf_s, buf_r = ((b2_send, b2), (c2_send, c2))[which]
        for p in range(4):
            for s in range(4):
                buf_s[h, p, s] = jnp.concatenate(
                    [total[q // 2, p, 4 * s:4 * s + 4, 128 * (q % 2):128 * (q % 2) + 128] for q in range(4)], axis=0).astype(bf16)
        for d in (2, 1, 3, 0):
            for s in range(4):
                if d:
                    final_copy(which, h, d, s).start()
                else:
                    @unless(final_self(d, s))
                    def _():
                        final_copy(which, h, d, s).start()

                    @pl.when(final_self(d, s))
                    def _():
                        buf_r[h, (first_pos[which] * 2 + zl) * 2 + zh] = buf_s[h, first_pos[which], s]

    @unless(zh == core)
    def _():
        arrived(arecv, col_r.at[2])

    @pl.when(zh == core)
    def _():
        arrived(arecv.at[0], col_r.at[2])

    sums = {}
    for which, h in order:
        buf_r = (b2, c2)[which]

        @unless(zh == core)
        def _():
            arrived(buf_r.at[h], f_r.at[which * 2 + h])

        @pl.when(zh == core)
        def _():
            arrived(buf_r.at[h, pl.ds(0, 15)], f_r.at[which * 2 + h])

        for t in range(2):
            total = sum(buf_r[h, 2 * k + t].astype(f32) for k in range(8))
            sums[which, h, t] = jnp.concatenate([total[4 * q:4 * q + 4] for q in range(4)], axis=1)
    steps = []
    for t in range(2):
        g = arecv[t]
        step = [learn_rate * (w[...] * jnp.concatenate([g[0:4], g[4:8]], axis=1))]
        for which in range(2):
            step.append(learn_rate * jnp.concatenate([sums[which, 0, t], sums[which, 1, t]], axis=1))
        steps.append(step)

    @pl.loop(0, 48)
    def _(attr):
        value = fac[attr]
        for t in range(2):
            step = jnp.where(tri[t, 2] == attr, steps[t][2], 0.0)
            for m in (1, 0):
                step = jnp.where(tri[t, m] == attr, steps[t][m], step)
            value = value - step
        out[attr] = value

    def left(ref, k):
        rcopy(ref, ref, sent.at[k], sent.at[k], 0, 0).wait_send()

    tg_copy.wait_send()
    left(scaled.at[0, pl.ds(0, 960)], 1)
    left(pm_send, 2)
    left(scaled.at[0, pl.ds(0, 768)], 3)

    @unless(zh == core)
    def _():
        left(scaled.at[0, pl.ds(0, 96)], 0)
        left(asend, 4)
        left(scaled.at[0, pl.ds(0, 256)], 5)

    @pl.when(zh == core)
    def _():
        left(scaled.at[0, pl.ds(0, 64)], 0)
        left(asend.at[0], 4)
        left(scaled.at[0, pl.ds(0, 240)], 5)


def on_device(factors, rank_weights, triples, targets):
    rows = rank_weights.shape[0]
    hw = rows // 2
    vmem = pl.BlockSpec(memory_space=pltpu.VMEM)
    hbm = pl.BlockSpec(memory_space=pl.ANY)
    dma = pltpu.SemaphoreType.DMA
    V = pltpu.VMEM
    return pl.pallas_call(
        kernel,
        out_shape=jax.ShapeDtypeStruct(factors.shape, f32),
        in_specs=[pl.BlockSpec(memory_space=pltpu.SMEM), vmem, hbm, hbm],
        out_specs=vmem,
        scratch_shapes=[
            V(factors.shape, f32),
            V((2, 16, hw), bf16),
            V((2, 16, hw), bf16),
            V((4, 16, hw), bf16),
            V((2, 16, hw), bf16),
            V((2, 4, 4, 16, hw), bf16),
            V((2, 4, 4, 16, hw), bf16),
            V((8, rows), f32),
            V((8, 256, 256), bf16),
            V((2, 2048, hw), bf16),
            V((8, 256, 256), f32),
            V((8, 256, 256), bf16),
            V((8, 256, 256), bf16),
            V((2048, 256), bf16),
            V((256, 2048), bf16),
            V((8, rows), f32),
            V((2, 2, 4, 4, 16, 256), f32),
            V((2, 2, 4, 4, 16, 256), f32),
            V((2, 2, 4, 4, 16, 256), bf16),
            V((2, 2, 4, 4, 16, 256), bf16),
            V((2, 3, 2, 4, 16, 256), bf16),
            V((2, 3, 2, 4, 16, 256), bf16),
            V((2, 4, 4, 16, 128), bf16),
            V((2, 4, 4, 16, 128), bf16),
            V((2, 16, 16, 128), bf16),
            V((2, 16, 16, 128), bf16),
            V((2, 8, hw), f32),
            V((2, 8, hw), f32),
            dma((2,)), dma((2,)), dma((6,)), dma((3,)), dma((6,)), dma((16,)), dma((4,)), dma((4,)), dma((4,)), dma((4,)),
        ],
        compiler_params=pltpu.CompilerParams(collective_id=0, has_side_effects=True, vmem_limit_bytes=56 * 1024 * 1024),
    )(triples, rank_weights.reshape(1, rows), factors, targets)


def solution(mesh):
    in_specs = (P(None, "cell", "rank"), P("rank"), P(), P(None, "cell", None, None))
    return jax.shard_map(on_device, mesh=mesh, in_specs=in_specs, out_specs=P(None, "cell", "rank"), check_vma=False)
```

```python
import jax
import jax.numpy as jnp
from jax import lax
from jax.experimental import pallas as pl
from jax.experimental.pallas import tpu as pltpu
from jax.sharding import PartitionSpec as P

learn_rate = 0.02
MESH = pl.DeviceIdType.MESH
f32, bf16 = jnp.float32, jnp.bfloat16
NT = (((1,), (1,)), ((), ()))


def cell_of(x, y, zl, core):
    return ((x * 4 + y) * 2 + zl) * 2 + core


def rcopy(src, dst, send_sem, recv_sem, cell, rank):
    return pltpu.make_async_remote_copy(
        src_ref=src, dst_ref=dst, send_sem=send_sem, recv_sem=recv_sem,
        device_id={"cell": cell, "rank": rank}, device_id_type=MESH)


def arrived(ref, sem):
    rcopy(ref, ref, sem, sem, 0, 0).wait_recv()


def unless(flag):
    return pl.when(jnp.logical_not(flag))


def kernel(tri, w, fac_hbm, tgt, steps, fac, msg, amsg, col, acol, bfull, cfull, wa, tg, scaled, pm_own, pm_send, pm_recv,
           resid, resid_t, ga, gb, gc, gb_send, gc_send, b1, c1, b2_send, c2_send, b2, c2, asend, arecv,
           l_sem, t_sem, sent, col_r, first_r, near_r, far_r, pm_r, r_r, f_r):
    cell = lax.axis_index("cell")
    zh = lax.axis_index("rank")
    core = cell % 2
    zl = (cell // 2) % 2
    y = (cell // 4) % 4
    x = cell // 16
    rows = w.shape[1]
    hw = rows // 2
    me = cell_of(x, y, zl, core)
    other = cell_of(x, y, zl, 1 - core)

    load = pltpu.make_async_copy(fac_hbm, fac, l_sem.at[0])
    load.start()
    own_tgt = pltpu.make_async_copy(tgt.at[zh], tg.at[pl.ds(core * 4, 4)], l_sem.at[1])
    own_tgt.start()

    barrier = pltpu.get_barrier_semaphore()

    def greet(to, rank):
        pl.semaphore_signal(barrier, inc=1, device_id={"cell": to, "rank": rank}, device_id_type=MESH)

    for s in range(4):
        @unless((zl == s // 2) & (core == s % 2) & (zh == core))
        def _():
            greet(cell_of(x, y, s // 2, s % 2), core)

    @pl.when(zh != core)
    def _():
        greet(other, zh)
    for d in range(1, 4):
        greet(cell_of((x + d) % 4, y, zl, core), zh)
        greet(cell_of(x, (y + d) % 4, zl, core), zh)

    load.wait()
    for t in range(2):
        a = w[...] * fac[tri[t, 0]]
        b = fac[tri[t, 1]]
        c = fac[tri[t, 2]]
        hi = a.astype(bf16).astype(f32)
        lo = a - hi
        msg[t] = jnp.concatenate([b[:, :hw], c[:, :hw], b[:, hw:], c[:, hw:]], axis=0).astype(bf16)
        amsg[t] = jnp.concatenate([hi[:, :hw], lo[:, :hw], hi[:, hw:], lo[:, hw:]], axis=0).astype(bf16)
    pl.semaphore_wait(barrier, 10)

    slot = zl * 2 + core

    def col_copy(t, dl):
        return rcopy(msg.at[t], col.at[slot], sent.at[0], col_r.at[0], cell_of(x, y, (zl + dl) % 2, zh), t)

    def acol_copy(t):
        return rcopy(amsg.at[t], acol.at[core], sent.at[0], col_r.at[1], cell_of(x, y, zl, zh), t)

    for dl in (1, 0):
        for t in range(2):
            if dl == 1:
                col_copy(t, dl).start()
            else:
                is_self = (core == zh) & (zh == t)

                @unless(is_self)
                def _():
                    col_copy(t, dl).start()

                @pl.when(is_self)
                def _():
                    col[slot] = msg[t]
                    acol[core] = amsg[t]

    @unless(core == zh)
    def _():
        arrived(col, col_r.at[0])

    @pl.when(core == zh)
    def _():
        arrived(col.at[pl.ds(0, 3)], col_r.at[0])

    got = [col[s].astype(f32) for s in range(4)]
    for h in range(2):
        bfull[h, x, y] = jnp.concatenate([m[8 * h:8 * h + 4] for m in got], axis=0).astype(bf16)
        cfull[h, x, y] = jnp.concatenate([m[8 * h + 4:8 * h + 8] for m in got], axis=0).astype(bf16)

    first_pos, second_pos = (x, y), (y, x)

    def block(which, h, p, q):
        return bfull.at[h, p, q] if which == 0 else cfull.at[h, q, p]

    def along_first(which, d):
        return cell_of((x + d) % 4, y, zl, core) if which == 0 else cell_of(x, (y + d) % 4, zl, core)

    def along_second(which, d):
        return along_first(1 - which, d)

    def send(which, h, p, q, recv_sem, to):
        view = block(which, h, p % 4, q % 4)
        rcopy(view, view, sent.at[1], recv_sem, to, zh).start()

    def first(which, d):
        view = block(which, slice(None), first_pos[which], second_pos[which])
        rcopy(view, view, sent.at[1], first_r.at[which * 3 + d - 1], along_first(which, d), zh).start()

    def first_wait(which, d):
        arrived(block(which, slice(None), (first_pos[which] + 4 - d) % 4, second_pos[which]), first_r.at[which * 3 + d - 1])

    def passed_on(h, e, up):
        return (e, up) in (((0, 1), (1, 1), (3, 0)), ((0, 0), (1, 1), (3, 0)))[h]

    def near_sem(which, h, e, up):
        return near_r.at[(which * 2 + h) * 4 + ((0, 1, None, 2)[e] if passed_on(h, e, up) else 3)]

    def near(which, h, e):
        for up in (1, 0):
            send(which, h, first_pos[which] + e, second_pos[which], near_sem(which, h, e, up), along_second(which, 1 if up else 3))
        if e == 2:
            send(which, h, first_pos[which] + e, second_pos[which], far_r.at[which * 2 + h], along_second(which, 2))

    def forward(which, h, e):
        up = 1 if passed_on(h, e, 1) else 0
        p, q = first_pos[which] + e, second_pos[which] + (3 if up else 1)
        arrived(block(which, h, p % 4, q % 4), near_sem(which, h, e, up))
        send(which, h, p, q, far_r.at[which * 2 + h], along_second(which, 1 if up else 3))

    both = [(which, h) for h in range(2) for which in range(2)]
    for d in (2, 1, 3):
        for which in range(2):
            first(which, d)
    for which, h in both:
        near(which, h, 0)
    for t in range(2):
        @unless((core == zh) & (zh == t))
        def _():
            acol_copy(t).start()

    tg_copy = rcopy(tgt.at[zh], tg.at[pl.ds(core * 4, 4)], t_sem.at[0], t_sem.at[1], other, zh)
    tg_copy.start()

    @unless(core == zh)
    def _():
        arrived(acol, col_r.at[1])

    @pl.when(core == zh)
    def _():
        arrived(acol.at[0], col_r.at[1])

    got = [acol[c].astype(f32) for c in range(2)]
    for h in range(2):
        wa[:, h * hw:(h + 1) * hw] = jnp.concatenate([m[8 * h:8 * h + 4] + m[8 * h + 4:8 * h + 8] for m in got], axis=0)

    for d in (1, 3, 2):
        for which in range(2):
            first_wait(which, d)
            near(which, 0, 4 - d)
            near(which, 1, 4 - d)
    for e in (0, 1, 3):
        for which, h in both:
            forward(which, h, e)

    def pm_copy(i):
        part = pl.ds(i, 2)
        return rcopy(pm_send.at[part], pm_recv.at[part], sent.at[2], pm_r.at[i // 2], other, zh)

    five = scaled.at[0, pl.ds(0, 80)]
    for h in range(2):
        for which in range(2):
            arrived(five, near_r.at[(which * 2 + h) * 4 + 3])
            arrived(bfull.at[h, 0], far_r.at[which * 2 + h])
        bs = bfull[h].reshape(256, hw).astype(f32)
        cs = cfull[h].reshape(256, hw)
        for i in range(8):
            s = (wa[i:i + 1, h * hw:(h + 1) * hw] * bs).astype(bf16)
            scaled[h, i * 256:(i + 1) * 256, :] = s
            pm = lax.dot_general(s, cs, NT, preferred_element_type=f32)
            if h == 0:
                pm_own[i] = pm
            else:
                pm = pm_own[i] + pm
                pm_own[i] = pm
                pm_send[i] = pm.astype(bf16)
                if i % 2:
                    pm_copy(i - 1).start()

    own_tgt.wait()
    arrived(tg.at[pl.ds((1 - core) * 4, 4)], t_sem.at[1])

    for i in range(8):
        if i % 2 == 0:
            arrived(pm_recv.at[pl.ds(i, 2)], pm_r.at[i // 2])
        r = (pm_own[i] + pm_recv[i].astype(f32) - tg[i].astype(f32)).astype(bf16)
        resid[i * 256:(i + 1) * 256, :] = r
        resid_t[:, i * 256:(i + 1) * 256] = r.T

    def scatter(src, dst, which, h, to):
        rcopy(src, dst, sent.at[3], r_r.at[which * 2 + h], to, zh).start()

    for h in range(2):
        for q in range(2):
            lanes = slice(q * 256, (q + 1) * 256)
            wlanes = slice(h * hw + q * 256, h * hw + (q + 1) * 256)
            part = jnp.dot(resid_t[...], scaled[h, :, lanes], preferred_element_type=f32).reshape(4, 4, 16, 256)
            gc[h, q] = part
            gc_send[h, q] = part.astype(bf16)
            for d in (2, 1, 3):
                scatter(gc_send.at[h, q, (x + d) % 4], c1.at[h, d - 1, q], 1, h, cell_of((x + d) % 4, y, zl, core))
            cs = cfull[h, :, :, :, lanes].reshape(256, 256)
            bs = bfull[h, :, :, :, lanes].reshape(256, 256).astype(f32)
            acc = jnp.zeros((256, 256), f32)
            for i in range(8):
                xprod = jnp.dot(resid[i * 256:(i + 1) * 256, :], cs, preferred_element_type=f32)
                ga[i:i + 1, wlanes] = jnp.sum(xprod * bs, axis=0, keepdims=True)
                acc = acc + wa[i:i + 1, wlanes] * xprod
            acc = acc.reshape(4, 4, 16, 256)
            gb[h, q] = acc
            gb_send[h, q] = acc.astype(bf16)
            for d in (2, 1, 3):
                scatter(gb_send.at[h, q, :, (y + d) % 4], b1.at[h, d - 1, q], 0, h, cell_of(x, (y + d) % 4, zl, core))

    def a_copy(c):
        return rcopy(asend.at[c], arecv.at[zh], sent.at[4], col_r.at[2], cell_of(x, y, zl, c), core)

    for c in range(2):
        asend[c] = jnp.concatenate([ga[4 * c:4 * c + 4, :hw], ga[4 * c:4 * c + 4, hw:]], axis=0)
        is_self = (core == c) & (zh == core)

        @unless(is_self)
        def _():
            a_copy(c).start()

        @pl.when(is_self)
        def _():
            arecv[zh] = asend[c]

    def final_copy(which, h, d, s):
        buf_s, buf_r = ((b2_send, b2), (c2_send, c2))[which]
        p = first_pos[which]
        if which == 0:
            to = cell_of((x + d) % 4, y, s // 2, s % 2)
        else:
            to = cell_of(x, (y + d) % 4, s // 2, s % 2)
        at = (p * 2 + zl) * 2 + zh
        return rcopy(buf_s.at[h, (p + d) % 4, s], buf_r.at[h, at], sent.at[5], f_r.at[which * 2 + h], to, core)

    def final_self(d, s):
        return (zl == s // 2) & (core == s % 2) & (zh == core) if d == 0 else None

    order = [(1, 0), (0, 0), (1, 1), (0, 1)]
    for which, h in order:
        buf, mine = (b1, gb[h, :, :, y]) if which == 0 else (c1, gc[h, :, x])
        arrived(buf.at[h], r_r.at[which * 2 + h])
        total = mine + buf[h, 0].astype(f32) + buf[h, 1].astype(f32) + buf[h, 2].astype(f32)
        buf_s, buf_r = ((b2_send, b2), (c2_send, c2))[which]
        for p in range(4):
            for s in range(4):
                buf_s[h, p, s] = jnp.concatenate(
                    [total[q // 2, p, 4 * s:4 * s + 4, 128 * (q % 2):128 * (q % 2) + 128] for q in range(4)], axis=0).astype(bf16)
        for d in (2, 1, 3, 0):
            for s in range(4):
                if d:
                    final_copy(which, h, d, s).start()
                else:
                    @unless(final_self(d, s))
                    def _():
                        final_copy(which, h, d, s).start()

                    @pl.when(final_self(d, s))
                    def _():
                        buf_r[h, (first_pos[which] * 2 + zl) * 2 + zh] = buf_s[h, first_pos[which], s]

    @unless(zh == core)
    def _():
        arrived(arecv, col_r.at[2])

    @pl.when(zh == core)
    def _():
        arrived(arecv.at[0], col_r.at[2])

    sums = {}
    for which, h in order:
        buf_r = (b2, c2)[which]

        @unless(zh == core)
        def _():
            arrived(buf_r.at[h], f_r.at[which * 2 + h])

        @pl.when(zh == core)
        def _():
            arrived(buf_r.at[h, pl.ds(0, 15)], f_r.at[which * 2 + h])

        for t in range(2):
            total = sum(buf_r[h, 2 * k + t].astype(f32) for k in range(8))
            sums[which, h, t] = jnp.concatenate([total[4 * q:4 * q + 4] for q in range(4)], axis=1)
    for t in range(2):
        g = arecv[t]
        steps[3 * t] = learn_rate * (w[...] * jnp.concatenate([g[0:4], g[4:8]], axis=1))
        for which in range(2):
            steps[3 * t + 1 + which] = learn_rate * jnp.concatenate([sums[which, 0, t], sums[which, 1, t]], axis=1)

    def left(ref, k):
        rcopy(ref, ref, sent.at[k], sent.at[k], 0, 0).wait_send()

    tg_copy.wait_send()
    left(scaled.at[0, pl.ds(0, 960)], 1)
    left(pm_send, 2)
    left(scaled.at[0, pl.ds(0, 768)], 3)

    @unless(zh == core)
    def _():
        left(scaled.at[0, pl.ds(0, 96)], 0)
        left(asend, 4)
        left(scaled.at[0, pl.ds(0, 256)], 5)

    @pl.when(zh == core)
    def _():
        left(scaled.at[0, pl.ds(0, 64)], 0)
        left(asend.at[0], 4)
        left(scaled.at[0, pl.ds(0, 240)], 5)


def update_kernel(tri, fac, steps, out):
    out[...] = fac[...]
    for t in range(2):
        for m in range(3):
            out[tri[t, m]] -= steps[3 * t + m]


def update(factors, triples, steps):
    vmem = pl.BlockSpec(memory_space=pltpu.VMEM)
    return pl.pallas_call(
        update_kernel,
        out_shape=jax.ShapeDtypeStruct(factors.shape, f32),
        in_specs=[pl.BlockSpec(memory_space=pltpu.SMEM), vmem, vmem],
        out_specs=vmem,
        compiler_params=pltpu.CompilerParams(vmem_limit_bytes=8 * 1024 * 1024),
    )(triples, factors, steps)


def on_device(factors, rank_weights, triples, targets):
    rows = rank_weights.shape[0]
    hw = rows // 2
    vmem = pl.BlockSpec(memory_space=pltpu.VMEM)
    hbm = pl.BlockSpec(memory_space=pl.ANY)
    dma = pltpu.SemaphoreType.DMA
    V = pltpu.VMEM
    steps = pl.pallas_call(
        kernel,
        out_shape=jax.ShapeDtypeStruct((6,) + factors.shape[1:], f32),
        in_specs=[pl.BlockSpec(memory_space=pltpu.SMEM), vmem, hbm, hbm],
        out_specs=vmem,
        scratch_shapes=[
            V(factors.shape, f32),
            V((2, 16, hw), bf16),
            V((2, 16, hw), bf16),
            V((4, 16, hw), bf16),
            V((2, 16, hw), bf16),
            V((2, 4, 4, 16, hw), bf16),
            V((2, 4, 4, 16, hw), bf16),
            V((8, rows), f32),
            V((8, 256, 256), bf16),
            V((2, 2048, hw), bf16),
            V((8, 256, 256), f32),
            V((8, 256, 256), bf16),
            V((8, 256, 256), bf16),
            V((2048, 256), bf16),
            V((256, 2048), bf16),
            V((8, rows), f32),
            V((2, 2, 4, 4, 16, 256), f32),
            V((2, 2, 4, 4, 16, 256), f32),
            V((2, 2, 4, 4, 16, 256), bf16),
            V((2, 2, 4, 4, 16, 256), bf16),
            V((2, 3, 2, 4, 16, 256), bf16),
            V((2, 3, 2, 4, 16, 256), bf16),
            V((2, 4, 4, 16, 128), bf16),
            V((2, 4, 4, 16, 128), bf16),
            V((2, 16, 16, 128), bf16),
            V((2, 16, 16, 128), bf16),
            V((2, 8, hw), f32),
            V((2, 8, hw), f32),
            dma((2,)), dma((2,)), dma((6,)), dma((3,)), dma((6,)), dma((16,)), dma((4,)), dma((4,)), dma((4,)), dma((4,)),
        ],
        compiler_params=pltpu.CompilerParams(collective_id=0, has_side_effects=True, vmem_limit_bytes=62 * 1024 * 1024),
    )(triples, rank_weights.reshape(1, rows), factors, targets)
    return update(factors, triples, steps)


def solution(mesh):
    in_specs = (P(None, "cell", "rank"), P("rank"), P(), P(None, "cell", None, None))
    return jax.shard_map(on_device, mesh=mesh, in_specs=in_specs, out_specs=P(None, "cell", "rank"), check_vma=False)
```

```python
import jax
import jax.numpy as jnp
from jax import lax
from jax.experimental import pallas as pl
from jax.experimental.pallas import tpu as pltpu
from jax.sharding import PartitionSpec as P

learn_rate = 0.02
MESH = pl.DeviceIdType.MESH
f32, bf16 = jnp.float32, jnp.bfloat16
NT = (((1,), (1,)), ((), ()))


def cell_of(x, y, zl, core):
    return ((x * 4 + y) * 2 + zl) * 2 + core


def rcopy(src, dst, send_sem, recv_sem, cell, rank):
    return pltpu.make_async_remote_copy(
        src_ref=src, dst_ref=dst, send_sem=send_sem, recv_sem=recv_sem,
        device_id={"cell": cell, "rank": rank}, device_id_type=MESH)


def arrived(ref, sem):
    rcopy(ref, ref, sem, sem, 0, 0).wait_recv()


def unless(flag):
    return pl.when(jnp.logical_not(flag))


def kernel(tri, w, fac_hbm, tgt, steps, fac, bmsg, cmsg, amsg, bcol, ccol, acol, bfull, cfull, wa, tg, tgh, scaled, pm,
           resid, resid_t, ga, gb, gc, gb_send, gc_send, gx_send, gx, b1, c1, b2_send, c2_send, b2, c2, asend, arecv,
           l_sem, t_sem, sent, col_r, first_r, second_r, cx_r, gx_r, r_r, f_r):
    cell = lax.axis_index("cell")
    zh = lax.axis_index("rank")
    core = cell % 2
    zl = (cell // 2) % 2
    y = (cell // 4) % 4
    x = cell // 16
    rows = w.shape[1]
    hw = rows // 2
    other = cell_of(x, y, zl, 1 - core)

    load = pltpu.make_async_copy(fac_hbm, fac, l_sem.at[0])
    load.start()
    own_tgt = pltpu.make_async_copy(tgt.at[zh], tg.at[pl.ds(core * 4, 4)], l_sem.at[1])
    own_tgt.start()

    barrier = pltpu.get_barrier_semaphore()

    def greet(to, rank):
        pl.semaphore_signal(barrier, inc=1, device_id={"cell": to, "rank": rank}, device_id_type=MESH)

    for k in range(1, 8):
        greet(cell_of(x, y, (zl + k // 4) % 2, (core + k // 2) % 2), (zh + k) % 2)
    for d in range(1, 4):
        greet(cell_of((x + d) % 4, y, zl, core), zh)
        greet(cell_of(x, (y + d) % 4, zl, core), zh)

    load.wait()
    for t in range(2):
        a = w[...] * fac[tri[t, 0]]
        b = fac[tri[t, 1]]
        c = fac[tri[t, 2]]
        bmsg[t] = jnp.concatenate([b[:, 256 * q:256 * q + 256] for q in range(4)], axis=0).astype(bf16)
        cmsg[t] = jnp.concatenate([c[:, 256 * q:256 * q + 256] for q in range(4)], axis=0).astype(bf16)
        amsg[t] = jnp.concatenate([a[:, :hw], a[:, hw:]], axis=0)
    pl.semaphore_wait(barrier, 13)

    def col_b(t, dl):
        return rcopy(bmsg.at[t], bcol.at[core * 2 + zh], sent.at[0], col_r.at[0], cell_of(x, y, (zl + dl) % 2, zl), t)

    def col_c(t, dl):
        return rcopy(cmsg.at[t], ccol.at[zl * 2 + core], sent.at[1], col_r.at[1], cell_of(x, y, (zl + dl) % 2, zh), t)

    def col_a(t, dc):
        return rcopy(amsg.at[t], acol.at[core * 2 + zh], sent.at[2], col_r.at[2], cell_of(x, y, zl, (core + dc) % 2), t)

    for t in range(2):
        c_self = (core == zh) & (zh == t)
        b_self = (core == zl) & (zh == t)

        @unless(c_self)
        def _():
            col_c(t, 0).start()

        @pl.when(c_self)
        def _():
            ccol[zl * 2 + core] = cmsg[t]

        @unless(b_self)
        def _():
            col_b(t, 0).start()

        @pl.when(b_self)
        def _():
            bcol[core * 2 + zh] = bmsg[t]

    def arrived_some(flag, ref, n, sem):
        @unless(flag)
        def _():
            arrived(ref, sem)

        @pl.when(flag)
        def _():
            arrived(ref.at[pl.ds(0, n)], sem)

    for t in range(2):
        col_c(t, 1).start()
        col_b(t, 1).start()
    arrived_some(core == zh, ccol, 3, col_r.at[1])
    got = [ccol[k].astype(f32) for k in range(4)]
    for h in range(2):
        cfull[core, h, x, y] = jnp.concatenate(
            [jnp.concatenate([m[4 * q:4 * q + 4] for m in got], axis=0) for q in (2 * h, 2 * h + 1)], axis=1).astype(bf16)

    def x_first(which, h):
        return which == h

    def first_pos(which, h):
        return x if x_first(which, h) else y

    def second_pos(which, h):
        return y if x_first(which, h) else x

    def block(which, h, p, q):
        bx, by = (p, q) if x_first(which, h) else (q, p)
        return bfull.at[h, bx, by] if which == 0 else cfull.at[core, h, bx, by]

    def along(along_x, d, l=zl, c=core):
        return cell_of((x + d) % 4, y, l, c) if along_x else cell_of(x, (y + d) % 4, l, c)

    def send(which, h, p, q, recv_sem, to):
        view = block(which, h, p % 4, q % 4)
        rcopy(view, view, sent.at[3], recv_sem, to, zh).start()

    def first_sem(which, h, d):
        return first_r.at[(which * 2 + h) * 3 + d - 1]

    def first(which, h, d):
        send(which, h, first_pos(which, h), second_pos(which, h), first_sem(which, h, d), along(x_first(which, h), d))

    def first_wait(which, h, d):
        arrived(block(which, h, (first_pos(which, h) + 4 - d) % 4, second_pos(which, h)), first_sem(which, h, d))

    def second(which, h, e):
        for d in (2, 1, 3):
            send(which, h, first_pos(which, h) + e, second_pos(which, h), second_r.at[which * 2 + h],
                 along(not x_first(which, h), d))

    def second_wait(which, h):
        arrived(scaled.at[0, 0, pl.ds(0, 192)], second_r.at[which * 2 + h])

    both = [(which, h) for which in (1, 0) for h in range(2)]
    for h in range(2):
        for d in (2, 1, 3):
            first(1, h, d)
    arrived_some(core == zl, bcol, 3, col_r.at[0])
    got = [bcol[2 * (k % 2) + k // 2].astype(f32) for k in range(4)]
    for h in range(2):
        bfull[h, x, y] = jnp.concatenate(
            [jnp.concatenate([m[4 * q:4 * q + 4] for m in got], axis=0) for q in (2 * h, 2 * h + 1)], axis=1).astype(bf16)
        for d in (2, 1, 3):
            first(0, h, d)
    for which, h in both:
        second(which, h, 0)

    for t in range(2):
        col_a(t, 1).start()
        a_self = zh == t

        @unless(a_self)
        def _():
            col_a(t, 0).start()

        @pl.when(a_self)
        def _():
            acol[core * 2 + zh] = amsg[t]
    tg_copy = rcopy(tgt.at[zh], tg.at[pl.ds(core * 4, 4)], t_sem.at[0], t_sem.at[1], other, zh)
    tg_copy.start()

    for which in (1, 0):
        for d in (1, 3, 2):
            for h in range(2):
                first_wait(which, h, d)
                second(which, h, 4 - d)
    arrived(acol.at[pl.ds(0, 3)], col_r.at[2])
    for rh in range(2):
        got = [acol[c * 2 + rh] for c in range(2)]
        for h in range(2):
            wa[rh, :, h * hw:(h + 1) * hw] = jnp.concatenate([m[4 * h:4 * h + 4] for m in got], axis=0)
    own_tgt.wait()
    arrived(tg.at[pl.ds((1 - core) * 4, 4)], t_sem.at[1])
    for i in range(8):
        parts = tg[i].astype(f32).reshape(16, 2, 8, 256)
        tgh[i * 128:(i + 1) * 128, :] = jnp.where(core == 0, parts[:, 0], parts[:, 1]).reshape(128, 256)

    def c_copy(h):
        return rcopy(cfull.at[core, h], cfull.at[core, h], sent.at[4], cx_r.at[h], other, zh)

    for h in range(2):
        second_wait(1, h)
        c_copy(h).start()

    def b_part(h, rh, lanes):
        parts = bfull[h, :, :, :, lanes].astype(f32).reshape(16, 2, 8, -1)
        return jnp.where(rh == 0, parts[:, 0], parts[:, 1]).reshape(128, -1)

    for rh, halves in ((core, (0,)), (core, (1,)), (1 - core, (0, 1))):
        if len(halves) == 1:
            second_wait(0, halves[0])
        else:
            for h in halves:
                arrived(cfull.at[rh, h], cx_r.at[h])
        bs = [b_part(h, rh, slice(0, hw)) for h in halves]
        cs = [cfull[rh, h].reshape(256, hw) for h in halves]
        for i in range(0, 8, 2):
            part = None
            at = slice(i * 128, (i + 2) * 128)
            for n, h in enumerate(halves):
                s = jnp.concatenate(
                    [wa[rh, k:k + 1, h * hw:(h + 1) * hw] * bs[n] for k in (i, i + 1)], axis=0).astype(bf16)
                scaled[rh, h, at, :] = s
                term = lax.dot_general(s, cs[n], NT, preferred_element_type=f32)
                part = term if part is None else part + term
            if halves == (0,):
                pm[at, :] = part
            elif halves == (1,):
                pm[at, :] += part
            else:
                r = (pm[at, :] + part - tgh[at, :]).astype(bf16)
                resid[at, :] = r
                resid_t[:, at] = r.T

    def scatter(which, h, q):
        src, dst = ((gb_send, b1), (gc_send, c1))[which]
        on_x = not x_first(which, h)
        for d in (2, 1, 3):
            view = src.at[h, q, (x + d) % 4] if on_x else src.at[h, q, :, (y + d) % 4]
            rcopy(view, dst.at[h, d - 1, q], sent.at[6], r_r.at[which * 2 + h], along(on_x, d), zh).start()

    def grad_b(h, q):
        lanes = slice(q * 256, (q + 1) * 256)
        wlanes = slice(h * hw + q * 256, h * hw + (q + 1) * 256)
        accs = []
        for rh in range(2):
            cs = cfull[rh, h, :, :, :, lanes].reshape(256, 256)
            bs = bfull[h, :, :, :, lanes].astype(f32).reshape(16, 2, 8, 256)[:, rh].reshape(128, 256)
            acc = jnp.zeros((128, 256), f32)
            for i in range(0, 8, 2):
                xprod = jnp.dot(resid[i * 128:(i + 2) * 128, :], cs, preferred_element_type=f32)
                for k in range(2):
                    xp = xprod[k * 128:(k + 1) * 128]
                    ga[rh, i + k:i + k + 1, wlanes] = jnp.sum(xp * bs, axis=0, keepdims=True)
                    acc = acc + wa[rh, i + k:i + k + 1, wlanes] * xp
            accs.append(acc.reshape(16, 1, 8, 256))
        part = jnp.concatenate(accs, axis=1).reshape(4, 4, 16, 256)
        gb[h, q] = part
        gb_send[h, q] = part.astype(bf16)
        scatter(0, h, q)

    def grad_c_other(h):
        gx_send[h] = jnp.dot(resid_t[...], scaled[1 - core, h], preferred_element_type=f32).astype(bf16)
        rcopy(gx_send.at[h], gx.at[h], sent.at[5], gx_r.at[h], other, zh).start()

    def grad_c(h):
        part = jnp.dot(resid_t[...], scaled[core, h], preferred_element_type=f32)
        arrived(gx.at[h], gx_r.at[h])
        for q in range(2):
            lanes = slice(q * 256, (q + 1) * 256)
            total = (part[:, lanes] + gx[h, :, lanes].astype(f32)).reshape(4, 4, 16, 256)
            gc[h, q] = total
            gc_send[h, q] = total.astype(bf16)
            scatter(1, h, q)

    grad_b(0, 0)
    grad_b(1, 0)
    grad_c_other(0)
    grad_c_other(1)
    grad_b(0, 1)
    grad_b(1, 1)
    grad_c(0)
    grad_c(1)

    def a_copy(k):
        return rcopy(asend.at[k], arecv.at[zh * 2 + core], sent.at[9], col_r.at[3], cell_of(x, y, zl, k % 2), k // 2)

    for k in range(4):
        g = ga[k // 2, 4 * (k % 2):4 * (k % 2) + 4, :]
        asend[k] = jnp.concatenate([g[:, :hw], g[:, hw:]], axis=0)
        is_self = (core == k % 2) & (zh == k // 2)

        @unless(is_self)
        def _():
            a_copy(k).start()

        @pl.when(is_self)
        def _():
            arecv[zh * 2 + core] = asend[k]

    bufs = ((b2_send, b2), (c2_send, c2))

    def final_copy(which, h, d, s):
        buf_s, buf_r = bufs[which]
        p = first_pos(which, h)
        if which == 0:
            to, rank = along(x_first(which, h), d, core, s % 2), s // 2
        else:
            to, rank = along(x_first(which, h), d, s // 2, s % 2), core
        return rcopy(buf_s.at[h, (p + d) % 4, s], buf_r.at[h, (p * 2 + zl) * 2 + zh], sent.at[7 + which],
                     f_r.at[which * 2 + h], to, rank)

    def final_self(which, s):
        if which == 0:
            return (core == zl) & (core == s % 2) & (zh == s // 2)
        return (zl == s // 2) & (core == s % 2) & (zh == core)

    order = [(0, 0), (0, 1), (1, 1), (1, 0)]
    for which, h in order:
        buf, g = ((b1, gb), (c1, gc))[which]
        mine = g[h, :, x] if not x_first(which, h) else g[h, :, :, y]
        arrived(buf.at[h], r_r.at[which * 2 + h])
        total = mine + buf[h, 0].astype(f32) + buf[h, 1].astype(f32) + buf[h, 2].astype(f32)
        buf_s, buf_r = bufs[which]
        for p in range(4):
            for s in range(4):
                buf_s[h, p, s] = jnp.concatenate(
                    [total[q // 2, p, 4 * s:4 * s + 4, 128 * (q % 2):128 * (q % 2) + 128] for q in range(4)],
                    axis=0).astype(bf16)
        for d in (2, 1, 3):
            for s in range(4):
                final_copy(which, h, d, s).start()
        for s in range(4):
            @unless(final_self(which, s))
            def _():
                final_copy(which, h, 0, s).start()

            @pl.when(final_self(which, s))
            def _():
                buf_r[h, (first_pos(which, h) * 2 + zl) * 2 + zh] = buf_s[h, first_pos(which, h), s]

    arrived(arecv.at[pl.ds(0, 3)], col_r.at[3])
    for t in range(2):
        g = arecv[2 * t] + arecv[2 * t + 1]
        steps[3 * t] = learn_rate * (w[...] * jnp.concatenate([g[0:4], g[4:8]], axis=1))
    for which, h in order:
        buf_r = bufs[which][1]
        arrived_some(core == (zl, zh)[which], buf_r.at[h], 15, f_r.at[which * 2 + h])
        for t in range(2):
            total = sum(buf_r[h, 2 * k + t].astype(f32) for k in range(8))
            steps[3 * t + 1 + which, :, h * hw:(h + 1) * hw] = learn_rate * jnp.concatenate(
                [total[4 * q:4 * q + 4] for q in range(4)], axis=1)

    def left(n, k):
        ref = pm.at[pl.ds(0, n)]
        rcopy(ref, ref, sent.at[k], sent.at[k], 0, 0).wait_send()

    def left_some(flag, n, fewer, k):
        @unless(flag)
        def _():
            left(n, k)

        @pl.when(flag)
        def _():
            left(fewer, k)

    tg_copy.wait_send()
    left_some(core == zl, 32, 24, 0)
    left_some(core == zh, 32, 24, 1)
    left(48, 2)
    left(960, 3)
    left(512, 4)
    left(512, 5)
    left(768, 6)
    left_some(core == zl, 128, 120, 7)
    left_some(core == zh, 128, 120, 8)
    left(48, 9)


def update_kernel(tri, fac, steps, out):
    out[...] = fac[...]
    for t in range(2):
        for m in range(3):
            out[tri[t, m]] -= steps[3 * t + m]


def update(factors, triples, steps):
    vmem = pl.BlockSpec(memory_space=pltpu.VMEM)
    return pl.pallas_call(
        update_kernel,
        out_shape=jax.ShapeDtypeStruct(factors.shape, f32),
        in_specs=[pl.BlockSpec(memory_space=pltpu.SMEM), vmem, vmem],
        out_specs=vmem,
        compiler_params=pltpu.CompilerParams(vmem_limit_bytes=8 * 1024 * 1024),
    )(triples, factors, steps)


def on_device(factors, rank_weights, triples, targets):
    rows = rank_weights.shape[0]
    hw = rows // 2
    vmem = pl.BlockSpec(memory_space=pltpu.VMEM)
    hbm = pl.BlockSpec(memory_space=pl.ANY)
    dma = pltpu.SemaphoreType.DMA
    V = pltpu.VMEM
    steps = pl.pallas_call(
        kernel,
        out_shape=jax.ShapeDtypeStruct((6,) + factors.shape[1:], f32),
        in_specs=[pl.BlockSpec(memory_space=pltpu.SMEM), vmem, hbm, hbm],
        out_specs=vmem,
        scratch_shapes=[
            V(factors.shape, f32),
            V((2, 16, 256), bf16),
            V((2, 16, 256), bf16),
            V((2, 8, hw), f32),
            V((4, 16, 256), bf16),
            V((4, 16, 256), bf16),
            V((4, 8, hw), f32),
            V((2, 4, 4, 16, hw), bf16),
            V((2, 2, 4, 4, 16, hw), bf16),
            V((2, 8, rows), f32),
            V((8, 256, 256), bf16),
            V((1024, 256), f32),
            V((2, 2, 1024, hw), bf16),
            V((1024, 256), f32),
            V((1024, 256), bf16),
            V((256, 1024), bf16),
            V((2, 8, rows), f32),
            V((2, 2, 4, 4, 16, 256), f32),
            V((2, 2, 4, 4, 16, 256), f32),
            V((2, 2, 4, 4, 16, 256), bf16),
            V((2, 2, 4, 4, 16, 256), bf16),
            V((2, 256, hw), bf16),
            V((2, 256, hw), bf16),
            V((2, 3, 2, 4, 16, 256), bf16),
            V((2, 3, 2, 4, 16, 256), bf16),
            V((2, 4, 4, 16, 128), bf16),
            V((2, 4, 4, 16, 128), bf16),
            V((2, 16, 16, 128), bf16),
            V((2, 16, 16, 128), bf16),
            V((4, 8, hw), f32),
            V((4, 8, hw), f32),
            dma((2,)), dma((2,)), dma((10,)), dma((4,)), dma((12,)), dma((4,)), dma((2,)), dma((2,)), dma((4,)), dma((4,)),
        ],
        compiler_params=pltpu.CompilerParams(collective_id=0, has_side_effects=True, vmem_limit_bytes=62 * 1024 * 1024),
    )(triples, rank_weights.reshape(1, rows), factors, targets)
    return update(factors, triples, steps)


def solution(mesh):
    in_specs = (P(None, "cell", "rank"), P("rank"), P(), P(None, "cell", None, None))
    return jax.shard_map(on_device, mesh=mesh, in_specs=in_specs, out_specs=P(None, "cell", "rank"), check_vma=False)
```

```python
import jax
import jax.numpy as jnp
from jax import lax
from jax.experimental import pallas as pl
from jax.experimental.pallas import tpu as pltpu
from jax.sharding import PartitionSpec as P

learn_rate = 0.02
MESH = pl.DeviceIdType.MESH
f32, bf16 = jnp.float32, jnp.bfloat16
NT = (((1,), (1,)), ((), ()))


def cell_of(x, y, zl, core):
    return ((x * 4 + y) * 2 + zl) * 2 + core


def rcopy(src, dst, send_sem, recv_sem, cell, rank):
    return pltpu.make_async_remote_copy(
        src_ref=src, dst_ref=dst, send_sem=send_sem, recv_sem=recv_sem,
        device_id={"cell": cell, "rank": rank}, device_id_type=MESH)


def arrived(ref, sem):
    rcopy(ref, ref, sem, sem, 0, 0).wait_recv()


def unless(flag):
    return pl.when(jnp.logical_not(flag))


def kernel(tri, w, fac_hbm, tgt, steps, fac, bmsg, cmsg, amsg, bcol, ccol, acol, bfull, cfull, wa, tg, tgh, scaled, pm,
           resid, resid_t, ga, gb, gc, gb_send, gc_send, gx_send, gx, b1, c1, b2_send, c2_send, b2, c2, asend, arecv,
           l_sem, t_sem, sent, col_r, first_r, second_r, cx_r, gx_r, r_r, f_r):
    cell = lax.axis_index("cell")
    zh = lax.axis_index("rank")
    core = cell % 2
    zl = (cell // 2) % 2
    y = (cell // 4) % 4
    x = cell // 16
    rows = w.shape[1]
    hw = rows // 2
    other = cell_of(x, y, zl, 1 - core)

    load = pltpu.make_async_copy(fac_hbm, fac, l_sem.at[0])
    load.start()
    own_tgt = pltpu.make_async_copy(tgt.at[zh], tg.at[pl.ds(core * 4, 4)], l_sem.at[1])
    own_tgt.start()

    barrier = pltpu.get_barrier_semaphore()

    def greet(to, rank):
        pl.semaphore_signal(barrier, inc=1, device_id={"cell": to, "rank": rank}, device_id_type=MESH)

    for k in range(1, 8):
        greet(cell_of(x, y, (zl + k // 4) % 2, (core + k // 2) % 2), (zh + k) % 2)
    for d in range(1, 4):
        greet(cell_of((x + d) % 4, y, zl, core), zh)
        greet(cell_of(x, (y + d) % 4, zl, core), zh)

    load.wait()
    for t in range(2):
        a = w[...] * fac[tri[t, 0]]
        b = fac[tri[t, 1]]
        c = fac[tri[t, 2]]
        bmsg[t] = jnp.concatenate([b[:, 256 * q:256 * q + 256] for q in range(4)], axis=0).astype(bf16)
        cmsg[t] = jnp.concatenate([c[:, 256 * q:256 * q + 256] for q in range(4)], axis=0).astype(bf16)
        amsg[t] = jnp.concatenate([a[:, :hw], a[:, hw:]], axis=0)
    pl.semaphore_wait(barrier, 13)

    def col_b(t, dl):
        return rcopy(bmsg.at[t], bcol.at[core * 2 + zh], sent.at[0], col_r.at[0], cell_of(x, y, (zl + dl) % 2, zl), t)

    def col_c(t, dl):
        return rcopy(cmsg.at[t], ccol.at[zl * 2 + core], sent.at[1], col_r.at[1], cell_of(x, y, (zl + dl) % 2, zh), t)

    def col_a(t, dc):
        return rcopy(amsg.at[t], acol.at[core * 2 + zh], sent.at[2], col_r.at[2], cell_of(x, y, zl, (core + dc) % 2), t)

    for t in range(2):
        c_self = (core == zh) & (zh == t)
        b_self = (core == zl) & (zh == t)

        @unless(c_self)
        def _():
            col_c(t, 0).start()

        @pl.when(c_self)
        def _():
            ccol[zl * 2 + core] = cmsg[t]

        @unless(b_self)
        def _():
            col_b(t, 0).start()

        @pl.when(b_self)
        def _():
            bcol[core * 2 + zh] = bmsg[t]

    def arrived_some(flag, ref, n, sem):
        @unless(flag)
        def _():
            arrived(ref, sem)

        @pl.when(flag)
        def _():
            arrived(ref.at[pl.ds(0, n)], sem)

    for t in range(2):
        col_c(t, 1).start()
        col_b(t, 1).start()
    arrived_some(core == zh, ccol, 3, col_r.at[1])
    got = [ccol[k].astype(f32) for k in range(4)]
    for h in range(2):
        cfull[core, h, x, y] = jnp.concatenate(
            [jnp.concatenate([m[4 * q:4 * q + 4] for m in got], axis=0) for q in (2 * h, 2 * h + 1)], axis=1).astype(bf16)

    def x_first(which, h):
        return which == h

    def first_pos(which, h):
        return x if x_first(which, h) else y

    def second_pos(which, h):
        return y if x_first(which, h) else x

    def block(which, h, p, q):
        bx, by = (p, q) if x_first(which, h) else (q, p)
        return bfull.at[h, bx, by] if which == 0 else cfull.at[core, h, bx, by]

    def along(along_x, d, l=zl, c=core):
        return cell_of((x + d) % 4, y, l, c) if along_x else cell_of(x, (y + d) % 4, l, c)

    def send(which, h, p, q, recv_sem, to):
        view = block(which, h, p % 4, q % 4)
        rcopy(view, view, sent.at[3], recv_sem, to, zh).start()

    def first_sem(which, h, d):
        return first_r.at[(which * 2 + h) * 3 + d - 1]

    def first(which, h, d):
        send(which, h, first_pos(which, h), second_pos(which, h), first_sem(which, h, d), along(x_first(which, h), d))

    def first_wait(which, h, d):
        arrived(block(which, h, (first_pos(which, h) + 4 - d) % 4, second_pos(which, h)), first_sem(which, h, d))

    def second(which, h, e):
        for d in (2, 1, 3):
            send(which, h, first_pos(which, h) + e, second_pos(which, h), second_r.at[which * 2 + h],
                 along(not x_first(which, h), d))

    def second_wait(which, h):
        arrived(scaled.at[0, 0, pl.ds(0, 192)], second_r.at[which * 2 + h])

    both = [(which, h) for which in (1, 0) for h in range(2)]
    for h in range(2):
        for d in (2, 1, 3):
            first(1, h, d)
    arrived_some(core == zl, bcol, 3, col_r.at[0])
    got = [bcol[2 * (k % 2) + k // 2].astype(f32) for k in range(4)]
    for h in range(2):
        bfull[h, x, y] = jnp.concatenate(
            [jnp.concatenate([m[4 * q:4 * q + 4] for m in got], axis=0) for q in (2 * h, 2 * h + 1)], axis=1).astype(bf16)
        for d in (2, 1, 3):
            first(0, h, d)
    for which, h in both:
        second(which, h, 0)

    for t in range(2):
        col_a(t, 1).start()
        a_self = zh == t

        @unless(a_self)
        def _():
            col_a(t, 0).start()

        @pl.when(a_self)
        def _():
            acol[core * 2 + zh] = amsg[t]
    tg_copy = rcopy(tgt.at[zh], tg.at[pl.ds(core * 4, 4)], t_sem.at[0], t_sem.at[1], other, zh)
    tg_copy.start()

    for which in (1, 0):
        for d in (1, 3, 2):
            for h in range(2):
                first_wait(which, h, d)
                second(which, h, 4 - d)
    arrived(acol.at[pl.ds(0, 3)], col_r.at[2])
    for rh in range(2):
        got = [acol[c * 2 + rh] for c in range(2)]
        for h in range(2):
            wa[rh, :, h * hw:(h + 1) * hw] = jnp.concatenate([m[4 * h:4 * h + 4] for m in got], axis=0)
    own_tgt.wait()
    arrived(tg.at[pl.ds((1 - core) * 4, 4)], t_sem.at[1])
    for i in range(8):
        parts = tg[i].astype(f32).reshape(16, 2, 8, 256)
        tgh[i * 128:(i + 1) * 128, :] = jnp.where(core == 0, parts[:, 0], parts[:, 1]).reshape(128, 256)

    def c_copy(h):
        return rcopy(cfull.at[core, h], cfull.at[core, h], sent.at[4], cx_r.at[h], other, zh)

    for h in range(2):
        second_wait(1, h)
        c_copy(h).start()

    def b_part(h, rh, lanes):
        parts = bfull[h, :, :, :, lanes].astype(f32).reshape(16, 2, 8, -1)
        return jnp.where(rh == 0, parts[:, 0], parts[:, 1]).reshape(128, -1)

    for rh, halves in ((core, (0,)), (core, (1,)), (1 - core, (0, 1))):
        if len(halves) == 1:
            second_wait(0, halves[0])
        else:
            for h in halves:
                arrived(cfull.at[rh, h], cx_r.at[h])
        bs = [b_part(h, rh, slice(0, hw)) for h in halves]
        cs = [cfull[rh, h].reshape(256, hw) for h in halves]
        for i in range(0, 8, 2):
            part = None
            at = slice(i * 128, (i + 2) * 128)
            for n, h in enumerate(halves):
                s = jnp.concatenate(
                    [wa[rh, k:k + 1, h * hw:(h + 1) * hw] * bs[n] for k in (i, i + 1)], axis=0).astype(bf16)
                scaled[rh, h, at, :] = s
                term = lax.dot_general(s, cs[n], NT, preferred_element_type=f32)
                part = term if part is None else part + term
            if halves == (0,):
                pm[at, :] = part
            elif halves == (1,):
                pm[at, :] += part
            else:
                r = (pm[at, :] + part - tgh[at, :]).astype(bf16)
                resid[at, :] = r
                resid_t[:, at] = r.T

    def scatter(which, h, q):
        src, dst = ((gb_send, b1), (gc_send, c1))[which]
        on_x = not x_first(which, h)
        for d in (2, 1, 3):
            view = src.at[h, q, (x + d) % 4] if on_x else src.at[h, q, :, (y + d) % 4]
            rcopy(view, dst.at[h, d - 1, q], sent.at[6], r_r.at[which * 2 + h], along(on_x, d), zh).start()

    def grad_b(h, q):
        lanes = slice(q * 256, (q + 1) * 256)
        wlanes = slice(h * hw + q * 256, h * hw + (q + 1) * 256)
        accs = []
        for rh in range(2):
            cs = cfull[rh, h, :, :, :, lanes].reshape(256, 256)
            bs = bfull[h, :, :, :, lanes].astype(f32).reshape(16, 2, 8, 256)[:, rh].reshape(128, 256)
            acc = jnp.zeros((128, 256), f32)
            for i in range(0, 8, 2):
                xprod = jnp.dot(resid[i * 128:(i + 2) * 128, :], cs, preferred_element_type=f32)
                for k in range(2):
                    xp = xprod[k * 128:(k + 1) * 128]
                    ga[rh, i + k:i + k + 1, wlanes] = jnp.sum(xp * bs, axis=0, keepdims=True)
                    acc = acc + wa[rh, i + k:i + k + 1, wlanes] * xp
            accs.append(acc.reshape(16, 1, 8, 256))
        part = jnp.concatenate(accs, axis=1).reshape(4, 4, 16, 256)
        gb[h, q] = part
        gb_send[h, q] = part.astype(bf16)
        scatter(0, h, q)

    def grad_c_other(h):
        gx_send[h] = jnp.dot(resid_t[...], scaled[1 - core, h], preferred_element_type=f32).astype(bf16)
        rcopy(gx_send.at[h], gx.at[h], sent.at[5], gx_r.at[h], other, zh).start()

    def grad_c(h):
        part = jnp.dot(resid_t[...], scaled[core, h], preferred_element_type=f32)
        arrived(gx.at[h], gx_r.at[h])
        for q in range(2):
            lanes = slice(q * 256, (q + 1) * 256)
            total = (part[:, lanes] + gx[h, :, lanes].astype(f32)).reshape(4, 4, 16, 256)
            gc[h, q] = total
            gc_send[h, q] = total.astype(bf16)
            scatter(1, h, q)

    grad_b(0, 0)
    grad_b(1, 0)
    grad_c_other(1)
    grad_c_other(0)
    grad_b(0, 1)
    grad_b(1, 1)
    grad_c(1)
    grad_c(0)

    def a_copy(k):
        return rcopy(asend.at[k], arecv.at[zh * 2 + core], sent.at[9], col_r.at[3], cell_of(x, y, zl, k % 2), k // 2)

    for k in range(4):
        g = ga[k // 2, 4 * (k % 2):4 * (k % 2) + 4, :]
        asend[k] = jnp.concatenate([g[:, :hw], g[:, hw:]], axis=0)
        is_self = (core == k % 2) & (zh == k // 2)

        @unless(is_self)
        def _():
            a_copy(k).start()

        @pl.when(is_self)
        def _():
            arecv[zh * 2 + core] = asend[k]

    bufs = ((b2_send, b2), (c2_send, c2))

    def final_copy(which, h, d, s):
        buf_s, buf_r = bufs[which]
        p = first_pos(which, h)
        if which == 0:
            to, rank = along(x_first(which, h), d, core, s % 2), s // 2
        else:
            to, rank = along(x_first(which, h), d, s // 2, s % 2), core
        return rcopy(buf_s.at[h, (p + d) % 4, s], buf_r.at[h, (p * 2 + zl) * 2 + zh], sent.at[7 + which],
                     f_r.at[which * 2 + h], to, rank)

    def final_self(which, s):
        if which == 0:
            return (core == zl) & (core == s % 2) & (zh == s // 2)
        return (zl == s // 2) & (core == s % 2) & (zh == core)

    order = [(0, 0), (0, 1), (1, 1), (1, 0)]
    for which, h in order:
        buf, g = ((b1, gb), (c1, gc))[which]
        mine = g[h, :, x] if not x_first(which, h) else g[h, :, :, y]
        arrived(buf.at[h], r_r.at[which * 2 + h])
        total = mine + buf[h, 0].astype(f32) + buf[h, 1].astype(f32) + buf[h, 2].astype(f32)
        buf_s, buf_r = bufs[which]
        for p in range(4):
            for s in range(4):
                buf_s[h, p, s] = jnp.concatenate(
                    [total[q // 2, p, 4 * s:4 * s + 4, 128 * (q % 2):128 * (q % 2) + 128] for q in range(4)],
                    axis=0).astype(bf16)
        for d in (2, 1, 3):
            for s in range(4):
                final_copy(which, h, d, s).start()
        for s in range(4):
            @unless(final_self(which, s))
            def _():
                final_copy(which, h, 0, s).start()

            @pl.when(final_self(which, s))
            def _():
                buf_r[h, (first_pos(which, h) * 2 + zl) * 2 + zh] = buf_s[h, first_pos(which, h), s]

    arrived(arecv.at[pl.ds(0, 3)], col_r.at[3])
    for t in range(2):
        g = arecv[2 * t] + arecv[2 * t + 1]
        steps[3 * t] = learn_rate * (w[...] * jnp.concatenate([g[0:4], g[4:8]], axis=1))
    for which, h in order:
        buf_r = bufs[which][1]
        arrived_some(core == (zl, zh)[which], buf_r.at[h], 15, f_r.at[which * 2 + h])
        for t in range(2):
            total = sum(buf_r[h, 2 * k + t].astype(f32) for k in range(8))
            steps[3 * t + 1 + which, :, h * hw:(h + 1) * hw] = learn_rate * jnp.concatenate(
                [total[4 * q:4 * q + 4] for q in range(4)], axis=1)

    def left(n, k):
        ref = pm.at[pl.ds(0, n)]
        rcopy(ref, ref, sent.at[k], sent.at[k], 0, 0).wait_send()

    def left_some(flag, n, fewer, k):
        @unless(flag)
        def _():
            left(n, k)

        @pl.when(flag)
        def _():
            left(fewer, k)

    tg_copy.wait_send()
    left_some(core == zl, 32, 24, 0)
    left_some(core == zh, 32, 24, 1)
    left(48, 2)
    left(960, 3)
    left(512, 4)
    left(512, 5)
    left(768, 6)
    left_some(core == zl, 128, 120, 7)
    left_some(core == zh, 128, 120, 8)
    left(48, 9)


def update_kernel(tri, fac, steps, out):
    out[...] = fac[...]
    for t in range(2):
        for m in range(3):
            out[tri[t, m]] -= steps[3 * t + m]


def update(factors, triples, steps):
    vmem = pl.BlockSpec(memory_space=pltpu.VMEM)
    return pl.pallas_call(
        update_kernel,
        out_shape=jax.ShapeDtypeStruct(factors.shape, f32),
        in_specs=[pl.BlockSpec(memory_space=pltpu.SMEM), vmem, vmem],
        out_specs=vmem,
        compiler_params=pltpu.CompilerParams(vmem_limit_bytes=8 * 1024 * 1024),
    )(triples, factors, steps)


def on_device(factors, rank_weights, triples, targets):
    rows = rank_weights.shape[0]
    hw = rows // 2
    vmem = pl.BlockSpec(memory_space=pltpu.VMEM)
    hbm = pl.BlockSpec(memory_space=pl.ANY)
    dma = pltpu.SemaphoreType.DMA
    V = pltpu.VMEM
    steps = pl.pallas_call(
        kernel,
        out_shape=jax.ShapeDtypeStruct((6,) + factors.shape[1:], f32),
        in_specs=[pl.BlockSpec(memory_space=pltpu.SMEM), vmem, hbm, hbm],
        out_specs=vmem,
        scratch_shapes=[
            V(factors.shape, f32),
            V((2, 16, 256), bf16),
            V((2, 16, 256), bf16),
            V((2, 8, hw), f32),
            V((4, 16, 256), bf16),
            V((4, 16, 256), bf16),
            V((4, 8, hw), f32),
            V((2, 4, 4, 16, hw), bf16),
            V((2, 2, 4, 4, 16, hw), bf16),
            V((2, 8, rows), f32),
            V((8, 256, 256), bf16),
            V((1024, 256), f32),
            V((2, 2, 1024, hw), bf16),
            V((1024, 256), f32),
            V((1024, 256), bf16),
            V((256, 1024), bf16),
            V((2, 8, rows), f32),
            V((2, 2, 4, 4, 16, 256), f32),
            V((2, 2, 4, 4, 16, 256), f32),
            V((2, 2, 4, 4, 16, 256), bf16),
            V((2, 2, 4, 4, 16, 256), bf16),
            V((2, 256, hw), bf16),
            V((2, 256, hw), bf16),
            V((2, 3, 2, 4, 16, 256), bf16),
            V((2, 3, 2, 4, 16, 256), bf16),
            V((2, 4, 4, 16, 128), bf16),
            V((2, 4, 4, 16, 128), bf16),
            V((2, 16, 16, 128), bf16),
            V((2, 16, 16, 128), bf16),
            V((4, 8, hw), f32),
            V((4, 8, hw), f32),
            dma((2,)), dma((2,)), dma((10,)), dma((4,)), dma((12,)), dma((4,)), dma((2,)), dma((2,)), dma((4,)), dma((4,)),
        ],
        compiler_params=pltpu.CompilerParams(collective_id=0, has_side_effects=True, vmem_limit_bytes=62 * 1024 * 1024),
    )(triples, rank_weights.reshape(1, rows), factors, targets)
    return update(factors, triples, steps)


def solution(mesh):
    in_specs = (P(None, "cell", "rank"), P("rank"), P(), P(None, "cell", None, None))
    return jax.shard_map(on_device, mesh=mesh, in_specs=in_specs, out_specs=P(None, "cell", "rank"), check_vma=False)
```
